32 devices in a mesh: parts: 2 (over y), space: 16 (over z, x, core).
Axes of the slice: x: 2, y: 2, z: 4, core: 2. Of those that a mesh axis runs over, the one named last changes fastest.
Arguments:
- outer_grad: bfloat16 [32, 4, 128, 1024], P(('parts', 'space')), parts along dimension 0, may hold values from -6 to 6
- block_input: bfloat16 [32, 4, 128, 1024], P(('parts', 'space')), parts along dimension 0, may hold values from -6 to 6
- third_input: bfloat16 [32, 4, 128, 1024], P(('parts', 'space')), parts along dimension 0, as said below
- second_input: bfloat16 [32, 8, 256, 256], P(('parts', 'space')), parts along dimension 0, as said below
- third_weight: bfloat16 [1024, 1024], replicated, may hold values from -0.1875 to 0.1875
- group_weight: bfloat16 [1024, 288], replicated, may hold values from -0.375 to 0.375
- first_weight: bfloat16 [1024, 1024], replicated, may hold values from -0.1875 to 0.1875
Outputs:
- input_grad: bfloat16 [32, 4, 128, 1024], P(('parts', 'space')), parts along dimension 0
- third_wgrad: float32 [2048, 1024], P(('parts', 'space')), parts along dimension 0
- group_wgrad: float32 [2048, 288], P(('parts', 'space')), parts along dimension 0
- first_wgrad: float32 [2048, 1024], P(('parts', 'space')), parts along dimension 0
The draws below stay inside these ranges and needn't reach their ends.
There are 2 independent parts, one for each index of `parts`. The reference program is written for one: setup_inputs(seed, part) draws one part's arguments, and reference() takes and returns one part's arrays. A program takes and returns all parts, laid end to end along the dimension named above; an argument that names none is the same for every part. Nothing has to cross between parts.
Inputs may be any that keep to these rules, and one draw needn't show every extreme that they name: `third_input`: rectified values: zero or positive, about half of them zero. `second_input`: rectified values: zero or positive, about half of them zero.
All inputs are finite; a program needn't handle non-finite values.
Results may differ from the reference program's by a relative error of at most 0.0049.
Values may be sent and summed in bfloat16 or wider, within the bound.
No kernel may reach another device: no remote copies, remote signals or barrier semaphores. Data moves between devices by JAX's collectives and lax.ppermute only.
A program may use at most 128 MiB of HBM per device.

```python
import math
import jax
import jax.numpy as jnp

C = 1024
GROUPS = 32
BH = 4
BW = 128
GW = 32
CS = 256
GRID_ROWS = 4
HEIGHT = 32
WIDTH = 256
POSITIONS = 8192
N_SPACE = 16


def rectified(key, shape):
    base_key, factor_key = jax.random.split(key)
    base = jnp.clip(jax.random.normal(base_key, shape, jnp.float32), -6.0, 6.0)
    factor = jnp.exp(jax.random.uniform(factor_key, shape, jnp.float32, math.log(0.5), math.log(2.0)))
    return (jnp.maximum(base, 0.0) * factor).astype(jnp.bfloat16)


def draw_third_input(key, part):
    return rectified(jax.random.fold_in(key, 31), (N_SPACE, BH, BW, C))


def draw_second_input(key, part):
    return rectified(jax.random.fold_in(key, 57), (N_SPACE, 2 * BH, 2 * BW, CS))


def raised(array, stream_key, source, target, shards_of, factor):
    owner, partner = [(jnp.arange(array.shape[position]) // (array.shape[position] // shards_of)).reshape([-1 if axis == position else 1 for axis in range(array.ndim)]) for position in (source, target)]
    chosen = jax.random.permutation(stream_key, shards_of)[partner]
    strong = (owner == chosen) | (owner == (partner + shards_of // 2) % shards_of)
    return jnp.where(strong, factor * array, array)


def block_scale(stream_key, extent, shards, smallest, largest):
    factor_of = 1.0
    for axis_at, blocks in shards:
        steps = jax.random.uniform(jax.random.fold_in(jax.random.fold_in(stream_key, 6), axis_at), (blocks,), jnp.float32, smallest / len(shards), largest / len(shards))
        factor_of = factor_of * jnp.repeat(jnp.exp(steps), extent[axis_at] // blocks).reshape((-1,) + (1,) * (len(extent) - 1 - axis_at))
    return factor_of


def noise(key, shape, deviation, bound, pieces=(), dtype=jnp.bfloat16):
    drawn = jax.random.normal(key, shape, jnp.float32) * deviation
    if len(pieces) > 0:
        drawn = block_scale(key, shape, pieces, -0.22, 0.18) * drawn
    return jnp.clip(drawn, min=-bound, max=bound).astype(dtype)


def bell_draw_with(own_key, dims, deviation, most, cuts, heavy, dtype=jnp.bfloat16):
    array = deviation * jax.random.normal(own_key, dims, jnp.float32)
    if cuts:
        array = array * block_scale(own_key, dims, cuts, -0.22, 0.18)
    return jnp.clip(raised(array, jax.random.fold_in(own_key, 3), *heavy), -most, most).astype(dtype)


def setup_inputs(seed: int = 0, part: int = 0) -> dict:
    key_of = jax.random.split(jax.random.key(seed), 8)
    part_keys = jax.random.split(jax.random.fold_in(key_of[7], part), 8)
    outer_grad = noise(part_keys[0], (N_SPACE, BH, BW, C), 1.0, 6.0, ((0, 16),))
    block_input = bell_draw_with(part_keys[1], (N_SPACE, BH, BW, C), 1.0, 6.0, ((0, 16),), (0, 3, 16, 2.0))
    third_input = draw_third_input(jax.random.fold_in(jax.random.fold_in(key_of[7], part), 71), part)
    second_input = draw_second_input(jax.random.fold_in(jax.random.fold_in(key_of[7], part), 71), part)
    third_weight = noise(key_of[4], (C, C), C ** -0.5, 0.1875)
    group_weight = noise(key_of[5], (C, 9 * GW), (9 * GW) ** -0.5, 0.375)
    first_weight = noise(key_of[6], (C, C), C ** -0.5, 0.1875)
    return dict(outer_grad=outer_grad, block_input=block_input, third_input=third_input, second_input=second_input, third_weight=third_weight, group_weight=group_weight, first_weight=first_weight)


def tiles_image(tiles):
    grid_rows = 2 * GRID_ROWS
    return tiles.reshape(grid_rows, 2, BH, BW, C).transpose(0, 2, 1, 3, 4).reshape(grid_rows * BH, 2 * BW, C)

def image_tiles(image):
    grid_rows = 2 * GRID_ROWS
    return image.reshape(grid_rows, BH, 2, BW, C).transpose(0, 2, 1, 3, 4).reshape(N_SPACE, BH, BW, C)

def blocks_image(blocks):
    shaped = blocks.reshape(GRID_ROWS, 2, 2, 2 * BH, 2 * BW, CS)
    return shaped.transpose(0, 3, 4, 1, 2, 5).reshape(HEIGHT, WIDTH, C)

def reference(outer_grad, block_input, third_input, second_input, third_weight, group_weight, first_weight):
    normalizer = 1.0 / math.sqrt(POSITIONS)
    grad_rows = tiles_image(outer_grad).reshape(POSITIONS, C)
    third_rows = tiles_image(third_input).reshape(POSITIONS, C)
    input_rows = tiles_image(block_input).reshape(POSITIONS, C)
    second_map = blocks_image(second_input)
    back_third = jnp.dot(grad_rows, third_weight.T, preferred_element_type=jnp.float32)
    inner_grad = jnp.where(third_rows > 0, back_third, 0.0).astype(jnp.bfloat16)
    third_wgrad = jnp.dot(third_rows.T, grad_rows, preferred_element_type=jnp.float32) * normalizer
    padded = jnp.pad(inner_grad.reshape(HEIGHT, WIDTH, C).astype(jnp.float32), ((1, 1), (1, 1), (0, 0)))
    kernel = group_weight.astype(jnp.float32).reshape(GROUPS, GW, 9, GW)
    second_groups = second_map.astype(jnp.float32).reshape(HEIGHT, WIDTH, GROUPS, GW)
    back_second = jnp.zeros((HEIGHT, WIDTH, GROUPS, GW), jnp.float32)
    tap_terms = []
    for tap_row in range(3):
        for tap_col in range(3):
            window = padded[2 - tap_row:2 - tap_row + HEIGHT, 2 - tap_col:2 - tap_col + WIDTH].reshape(HEIGHT, WIDTH, GROUPS, GW)
            back_second = back_second + jnp.einsum('hwgo,goi->hwgi', window, kernel[:, :, 3 * tap_row + tap_col, :])
            tap_terms.append(jnp.einsum('hwgi,hwgo->goi', second_groups, window))
    group_wgrad = jnp.stack(tap_terms, 2).reshape(C, 9 * GW) * normalizer
    first_map = jnp.where(second_map > 0, back_second.reshape(HEIGHT, WIDTH, C), 0.0).astype(jnp.bfloat16)
    first_rows = first_map.reshape(POSITIONS, C)
    first_wgrad = jnp.dot(input_rows.T, first_rows, preferred_element_type=jnp.float32) * normalizer
    summed = jnp.dot(first_rows, first_weight.T, preferred_element_type=jnp.float32) + grad_rows.astype(jnp.float32)
    input_grad = image_tiles(summed.astype(jnp.bfloat16).reshape(HEIGHT, WIDTH, C))
    return (input_grad, third_wgrad, group_wgrad, first_wgrad)
```

```python
import math

import jax
import jax.numpy as jnp
from jax import lax
from jax.experimental import pallas as pl
from jax.experimental.pallas import tpu as pltpu
from jax.sharding import PartitionSpec as P

BF = jnp.bfloat16
F32 = jnp.float32
VMEM_LIMIT = 48 * 1024 * 1024


def exchange(array, bit):
    count = lax.axis_size("space")
    return lax.ppermute(array, "space", [(i, i ^ (1 << bit)) for i in range(count)])


def exchange_across(array):
    count = lax.axis_size("space")
    route = []
    for low in range(count):
        high = low + 2
        if low & 2 and high < count:
            route += [(low, high), (high, low)]
    return lax.ppermute(array, "space", route)


def pick(array, index, axis):
    return lax.dynamic_index_in_dim(array, index, axis, keepdims=False)


def scatter_sum(total, bits, order, left):
    left = list(left)
    for bit in order:
        at = left.index(bit)
        left.pop(at)
        received = exchange(pick(total, 1 - bits[bit], at).astype(BF), bit)
        total = pick(total, bits[bit], at) + received.astype(F32)
    return total


def nt_dot(a, b):
    return lax.dot_general(a, b, (((1,), (1,)), ((), ())), preferred_element_type=F32)


def inner_kernel(grad_ref, weight_ref, mask_ref, out_ref):
    back = nt_dot(grad_ref[...], weight_ref[...])
    out_ref[...] = jnp.where(mask_ref[...] > 0, back, 0.0).astype(BF)


def inner_of(grad_rows, third_weight, third_rows):
    rows, channels = grad_rows.shape
    step = 256
    return pl.pallas_call(
        inner_kernel,
        grid=(channels // step,),
        in_specs=[
            pl.BlockSpec((rows, channels), lambda j: (0, 0)),
            pl.BlockSpec((step, channels), lambda j: (j, 0)),
            pl.BlockSpec((rows, step), lambda j: (0, j)),
        ],
        out_specs=pl.BlockSpec((rows, step), lambda j: (0, j)),
        out_shape=jax.ShapeDtypeStruct((rows, channels), BF),
        compiler_params=pltpu.CompilerParams(vmem_limit_bytes=VMEM_LIMIT),
        cost_estimate=pl.CostEstimate(
            flops=2 * rows * channels * channels, bytes_accessed=5 << 20, transcendentals=0
        ),
        name="inner",
    )(grad_rows, third_weight, third_rows)


def result_kernel(first_ref, weight_ref, grad_ref, out_ref):
    summed = nt_dot(first_ref[...], weight_ref[...])
    out_ref[...] = (summed + grad_ref[...].astype(F32)).astype(BF)


def result_of(first_rows, first_weight, grad_rows):
    rows, channels = grad_rows.shape
    step = 256
    return pl.pallas_call(
        result_kernel,
        grid=(channels // step,),
        in_specs=[
            pl.BlockSpec((rows, channels), lambda j: (0, 0)),
            pl.BlockSpec((step, channels), lambda j: (j, 0)),
            pl.BlockSpec((rows, step), lambda j: (0, j)),
        ],
        out_specs=pl.BlockSpec((rows, step), lambda j: (0, j)),
        out_shape=jax.ShapeDtypeStruct((rows, channels), BF),
        compiler_params=pltpu.CompilerParams(vmem_limit_bytes=VMEM_LIMIT),
        cost_estimate=pl.CostEstimate(
            flops=2 * rows * channels * channels, bytes_accessed=5 << 20, transcendentals=0
        ),
        name="result",
    )(first_rows, first_weight, grad_rows)


def spread_kernel(gw, taps, weight_ref, out_ref):
    step = weight_ref.shape[0]
    weight = weight_ref[...]
    source = lax.broadcasted_iota(jnp.int32, (taps * gw, step), 0)
    column = lax.broadcasted_iota(jnp.int32, (taps * gw, step), 1) % gw
    row_group = lax.broadcasted_iota(jnp.int32, (step, step), 0) // gw
    column_group = lax.broadcasted_iota(jnp.int32, (step, step), 1) // gw
    for tap in range(taps):
        chooser = jnp.where(source == tap * gw + column, 1.0, 0.0).astype(BF)
        copies = jnp.dot(weight, chooser, preferred_element_type=F32)
        out_ref[0, tap] = jnp.where(row_group == column_group, copies, 0.0).astype(BF)


def spread_of(group_weight, step):
    channels, width = group_weight.shape
    taps = 9
    gw = width // taps
    return pl.pallas_call(
        lambda w, o: spread_kernel(gw, taps, w, o),
        grid=(channels // step,),
        in_specs=[pl.BlockSpec((step, width), lambda j: (j, 0))],
        out_specs=pl.BlockSpec((1, taps, step, step), lambda j: (j, 0, 0, 0)),
        out_shape=jax.ShapeDtypeStruct((channels // step, taps, step, step), BF),
        compiler_params=pltpu.CompilerParams(vmem_limit_bytes=VMEM_LIMIT),
        name="spread",
    )(group_weight)


def conv_kernel(
    gw,
    piece,
    where_ref,
    inner_ref,
    top_ref,
    bottom_ref,
    edge_ref,
    second_ref,
    spread_ref,
    keep_in_ref,
    send_in_ref,
    first_ref,
    keep_ref,
    send_ref,
    group_keep_ref,
    group_send_ref,
    window_ref,
    term_ref,
):
    tile_rows, width, step = inner_ref.shape
    positions = tile_rows * width
    taps = spread_ref.shape[1]
    core = where_ref[0]
    at = lax.broadcasted_iota(jnp.int32, (width, step), 0)
    for row in range(tile_rows + 2):
        if row == 0:
            line = top_ref[...]
        elif row == tile_rows + 1:
            line = bottom_ref[...]
        else:
            line = inner_ref[row - 1]
        here = pl.ds(row * width, width)
        wide = line.astype(F32)
        edge = edge_ref[row : row + 1, :]
        left = jnp.where(core == 1, edge, 0.0)
        right = jnp.where(core == 0, edge, 0.0)
        window_ref[1, here, :] = line
        window_ref[2, here, :] = jnp.where(at == 0, left, pltpu.roll(wide, 1, 0)).astype(BF)
        window_ref[0, here, :] = jnp.where(
            at == width - 1, right, pltpu.roll(wide, width - 1, 0)
        ).astype(BF)
    second = second_ref[0]
    flipped = second.T
    lane_group = lax.broadcasted_iota(jnp.int32, (gw, step), 1) // gw
    back = jnp.zeros((positions, step), F32)
    for tap in range(taps):
        window = window_ref[tap % 3, pl.ds((2 - tap // 3) * width, positions), :]
        back = back + jnp.dot(window, spread_ref[0, tap], preferred_element_type=F32)
        term = jnp.dot(flipped, window, preferred_element_type=F32)
        mine = jnp.zeros((gw, step), F32)
        for group in range(step // gw):
            mine = jnp.where(lane_group == group, term[group * gw : (group + 1) * gw], mine)
        term_ref[tap * gw : (tap + 1) * gw, :] = mine
    first = jnp.where(second > 0, back, 0.0).astype(BF)
    first_ref[...] = first
    keep_ref[...] = jnp.dot(keep_in_ref[...], first, preferred_element_type=F32)
    send_ref[...] = jnp.dot(send_in_ref[...], first, preferred_element_type=F32).astype(BF)
    turned = term_ref[...].T.reshape(step // (2 * piece), 2, piece, taps * gw)
    low = turned[:, 0].reshape(step // 2, taps * gw)
    high = turned[:, 1].reshape(step // 2, taps * gw)
    group_keep_ref[...] = jnp.where(core == 0, low, high)
    group_send_ref[...] = jnp.where(core == 0, high, low).astype(BF)


def conv_of(where, inner, top, bottom, edge, second, spread, keep_in, send_in, gw, piece):
    tile_rows, width, channels = inner.shape
    slots, positions, step = second.shape
    taps = spread.shape[1]
    rows = keep_in.shape[0]
    grid_spec = pltpu.PrefetchScalarGridSpec(
        num_scalar_prefetch=1,
        grid=(slots,),
        in_specs=[
            pl.BlockSpec((tile_rows, width, step), lambda q, w: (0, 0, w[q + 1])),
            pl.BlockSpec((width, step), lambda q, w: (0, w[q + 1])),
            pl.BlockSpec((width, step), lambda q, w: (0, w[q + 1])),
            pl.BlockSpec((edge.shape[0], step), lambda q, w: (0, w[q + 1])),
            pl.BlockSpec((1, positions, step), lambda q, w: (q, 0, 0)),
            pl.BlockSpec((1, taps, step, step), lambda q, w: (w[q + 1], 0, 0, 0)),
            pl.BlockSpec((rows, positions), lambda q, w: (0, 0)),
            pl.BlockSpec((rows, positions), lambda q, w: (0, 0)),
        ],
        out_specs=[
            pl.BlockSpec((positions, step), lambda q, w: (0, w[q + 1])),
            pl.BlockSpec((rows, step), lambda q, w: (0, w[q + 1])),
            pl.BlockSpec((rows, step), lambda q, w: (0, w[q + 1])),
            pl.BlockSpec((step // 2, taps * gw), lambda q, w: (w[q + 1], 0)),
            pl.BlockSpec((step // 2, taps * gw), lambda q, w: (w[q + 1], 0)),
        ],
        scratch_shapes=[
            pltpu.VMEM((3, (tile_rows + 2) * width, step), BF),
            pltpu.VMEM((taps * gw, step), F32),
        ],
    )
    flops = 2 * slots * positions * step * (2 * taps * step + 2 * rows)
    return pl.pallas_call(
        lambda *refs: conv_kernel(gw, piece, *refs),
        grid_spec=grid_spec,
        out_shape=[
            jax.ShapeDtypeStruct((positions, channels), BF),
            jax.ShapeDtypeStruct((rows, channels), F32),
            jax.ShapeDtypeStruct((rows, channels), BF),
            jax.ShapeDtypeStruct((channels // 2, taps * gw), F32),
            jax.ShapeDtypeStruct((channels // 2, taps * gw), BF),
        ],
        compiler_params=pltpu.CompilerParams(vmem_limit_bytes=VMEM_LIMIT),
        cost_estimate=pl.CostEstimate(flops=flops, bytes_accessed=16 << 20, transcendentals=0),
        name="conv",
    )(where, inner, top, bottom, edge, second, spread, keep_in, send_in)


def per_device(
    outer_grad, block_input, third_input, second_input, third_weight, group_weight, first_weight
):
    devices = lax.axis_size("space")
    position = lax.axis_index("space")
    n_bits = devices.bit_length() - 1
    bits = [(position >> b) & 1 for b in range(n_bits)]
    core, half = bits[0], bits[1]
    _, tile_rows, width, channels = outer_grad.shape
    positions = tile_rows * width
    shard = channels // 4
    gw = group_weight.shape[1] // 9
    piece = channels // devices
    normalizer = 1.0 / math.sqrt(positions * devices)
    grad_rows = outer_grad.reshape(positions, channels)
    third_rows = third_input.reshape(positions, channels)
    input_rows = block_input.reshape(positions, channels)
    high_to_low = list(range(n_bits - 1, -1, -1))
    z_first = [*range(2, n_bits), 1]
    x_first = [*range(1, n_bits)]

    block = second_input[0].reshape(2, tile_rows, 2 * width, shard)
    far_sent = pick(block, 1 - half, 0)
    near = pick(block, half, 0).reshape(tile_rows, 2, width, shard)
    far = exchange(far_sent, 1).reshape(tile_rows, 2, width, shard)
    near_other = exchange(pick(near, 1 - core, 1), 0)
    far_other = exchange(pick(far, 1 - core, 1), 0)
    second = jnp.stack([pick(near, core, 1), near_other, pick(far, core, 1), far_other])
    second = second.reshape(4, positions, shard)
    where = jnp.stack(
        [
            core,
            2 * half + core,
            2 * half + 1 - core,
            2 * (1 - half) + core,
            2 * (1 - half) + 1 - core,
        ]
    ).astype(jnp.int32)

    by_core = third_rows.reshape(positions, channels // (2 * piece), 2, piece)
    third_keep = pick(by_core, core, 2).reshape(positions, channels // 2)
    third_send = pick(by_core, 1 - core, 2).reshape(positions, channels // 2)
    tn = (((0,), (0,)), ((), ()))
    sent = lax.dot_general(third_send, grad_rows, tn, preferred_element_type=F32).astype(BF)
    kept = lax.dot_general(third_keep, grad_rows, tn, preferred_element_type=F32)
    third_total = kept + exchange(sent, 0).astype(F32)
    third_total = third_total.reshape([2] * (n_bits - 1) + [piece, channels])
    third_wgrad = scatter_sum(third_total, bits, z_first, high_to_low[:-1]) * normalizer

    inner = inner_of(grad_rows, third_weight, third_rows).reshape(tile_rows, width, channels)
    inside = exchange(jnp.where(half == 0, inner[-1], inner[0]), 1)
    outside = exchange_across(jnp.where(half == 0, inner[0], inner[-1]))
    top = jnp.where(half == 0, outside, inside)
    bottom = jnp.where(half == 0, inside, outside)
    column = (1 - core) * (width - 1)
    edge = jnp.concatenate(
        [
            lax.dynamic_slice_in_dim(top, column, 1, 0),
            lax.dynamic_slice_in_dim(inner, column, 1, 1)[:, 0],
            lax.dynamic_slice_in_dim(bottom, column, 1, 0),
        ]
    )
    edge = exchange(edge, 0).astype(F32)

    spread = spread_of(group_weight, shard)
    turned = input_rows.T.reshape(channels // (2 * piece), 2, piece, positions)
    keep_in = pick(turned, core, 1).reshape(channels // 2, positions)
    send_in = pick(turned, 1 - core, 1).reshape(channels // 2, positions)
    first, kept, sent, group_kept, group_sent = conv_of(
        where, inner, top, bottom, edge, second, spread, keep_in, send_in, gw, piece
    )
    cut = 3 * channels // 8
    received = exchange(jnp.concatenate([group_sent, sent], 1), 0).astype(F32)
    total = jnp.concatenate([group_kept, kept], 1) + received
    cut += group_kept.shape[1]
    shape = [2] * (n_bits - 1) + [piece]
    one = scatter_sum(total[:, :cut].reshape([*shape, -1]), bits, z_first, high_to_low[:-1])
    two = scatter_sum(total[:, cut:].reshape([*shape, -1]), bits, x_first, high_to_low[:-1])
    total = jnp.concatenate([one, two], 1) * normalizer
    group_wgrad = total[:, : 9 * gw]
    first_wgrad = total[:, 9 * gw :]
    input_grad = result_of(first, first_weight, grad_rows).reshape(outer_grad.shape)
    return (input_grad, third_wgrad, group_wgrad, first_wgrad)


def solution(mesh):
    tiles = P(("parts", "space"), None, None, None)
    rows = P(("parts", "space"), None)
    return jax.shard_map(
        per_device,
        mesh=mesh,
        in_specs=(tiles, tiles, tiles, tiles, P(), P(), P()),
        out_specs=(tiles, rows, rows, rows),
        check_vma=False,
    )
```

```python
import math

import jax
import jax.numpy as jnp
from jax import lax
from jax.experimental import pallas as pl
from jax.experimental.pallas import tpu as pltpu
from jax.sharding import PartitionSpec as P

BF = jnp.bfloat16
F32 = jnp.float32
TAPS = 9
ROWS = 4


def exchange(array, bit):
    count = lax.axis_size("space")
    return lax.ppermute(array, "space", [(i, i ^ (1 << bit)) for i in range(count)])


def exchange_across(array):
    count = lax.axis_size("space")
    route = []
    for low in range(count):
        high = low + 2
        if low & 2 and high < count:
            route += [(low, high), (high, low)]
    return lax.ppermute(array, "space", route)


def after(value, *others):
    return lax.optimization_barrier((value, *others))[0]


def call(kernel, name, place, operands, outs, scratch=(), megabytes=12, pinned=True):
    inputs, specs = [], [pl.BlockSpec(memory_space=pltpu.SMEM)]
    for operand in operands:
        if isinstance(operand, tuple):
            inputs.append(pltpu.with_memory_space_constraint(operand[0], pltpu.HBM))
            specs.append(pl.BlockSpec(memory_space=pltpu.HBM))
        else:
            inputs.append(operand)
            specs.append(pl.BlockSpec(memory_space=pltpu.VMEM))
    kind = pltpu.VMEM if pinned else jax.ShapeDtypeStruct
    return pl.pallas_call(
        kernel,
        in_specs=specs,
        out_specs=[pl.BlockSpec(memory_space=pltpu.VMEM)] * len(outs),
        out_shape=[kind(*out) for out in outs],
        scratch_shapes=scratch,
        compiler_params=pltpu.CompilerParams(vmem_limit_bytes=megabytes * 1024 * 1024),
        cost_estimate=pl.CostEstimate(flops=0, bytes_accessed=0, transcendentals=0),
        name=name,
    )(place, *inputs)


def nt_dot(a, b):
    return lax.dot_general(a, b, (((1,), (1,)), ((), ())), preferred_element_type=F32)


def halves(value, bit):
    low, high = value[:, 0], value[:, 1]
    return jnp.where(bit == 0, low, high), jnp.where(bit == 0, high, low)


def pack_kernel(
    place_ref, second_ref, grad_ref, mask_ref,
    near_own_ref, near_core_ref, far_ref, edge_ref, grads_ref, masks_ref, sems,
):
    rows, width, _ = near_own_ref.shape
    core, half = place_ref[0], place_ref[1]
    edge_at = (1 - core) * (width - 16)
    copies = []
    for row in range(ROWS):
        there = pl.ds(pl.multiple_of(row * width + edge_at, 16), 16)
        copies.append((grad_ref.at[there], grads_ref.at[row]))
        copies.append((mask_ref.at[there], masks_ref.at[row]))
    for target, row_at, column_at in (
        (far_ref.at[0], 1 - half, core),
        (far_ref.at[1], 1 - half, 1 - core),
        (near_core_ref, half, 1 - core),
        (near_own_ref, half, core),
    ):
        source = second_ref.at[0, pl.ds(row_at * rows, rows), pl.ds(column_at * width, width)]
        copies.append((source, target))
    copies = [pltpu.make_async_copy(*pair, sems.at[at]) for at, pair in enumerate(copies)]
    for copy in copies:
        copy.start()
    for copy in copies:
        copy.wait()
    lines = []
    for buffer in (grads_ref, masks_ref):
        for row in range(ROWS):
            value = buffer[row].astype(F32)
            lines.append(jnp.where(core == 0, value[15:16], value[0:1]))
    lines += [jnp.zeros_like(lines[0])] * (16 - 2 * ROWS)
    edge_ref[...] = jnp.concatenate(lines).astype(BF)


def pack_of(place, second_input, grad_rows, third_rows):
    _, rows, columns, shard = second_input.shape
    channels = grad_rows.shape[1]
    out = (rows // 2, columns // 2, shard)
    return call(
        pack_kernel,
        "pack",
        place,
        [(second_input,), (grad_rows,), (third_rows,)],
        [(out, BF), (out, BF), ((2, *out), BF), ((16, channels), BF)],
        [
            pltpu.VMEM((ROWS, 16, channels), BF),
            pltpu.VMEM((ROWS, 16, channels), BF),
            pltpu.SemaphoreType.DMA((4 + 2 * ROWS,)),
        ],
    )


def inner_kernel(
    place_ref, grad_ref, weight_ref, mask_ref, edge_ref,
    out_ref, rim_ref, inside_ref, outside_ref,
):
    channels = weight_ref.shape[0]
    step = channels // 2
    width = grad_ref.shape[0] // ROWS
    half = place_ref[1]
    for part in range(2):
        here = slice(part * step, (part + 1) * step)
        weight = weight_ref[here, :]
        back = nt_dot(grad_ref[...], weight)
        inner = jnp.where(mask_ref[:, here] > 0, back, 0.0).astype(BF)
        out_ref[:, here] = inner
        beside = nt_dot(edge_ref[...], weight)
        kept = edge_ref[:, here].astype(F32)
        lines = [
            jnp.where(kept[ROWS + row : ROWS + row + 1] > 0, beside[row : row + 1], 0.0)
            for row in range(ROWS)
        ]
        nothing = [jnp.zeros_like(lines[0])]
        rim_ref[:, here] = jnp.concatenate(lines + nothing * (16 - ROWS)).astype(BF)
        first, last = inner[:width], inner[(ROWS - 1) * width :]
        upper = jnp.concatenate([lines[0]] + nothing * 15).astype(BF)
        lower = jnp.concatenate([lines[-1]] + nothing * 15).astype(BF)
        inside_ref[:width, here] = jnp.where(half == 0, last, first)
        inside_ref[width:, here] = jnp.where(half == 0, lower, upper)
        outside_ref[:width, here] = jnp.where(half == 0, first, last)
        outside_ref[width:, here] = jnp.where(half == 0, upper, lower)


def inner_of(place, grad_rows, third_weight, third_rows, edge):
    rows, channels = grad_rows.shape
    rim = ((rows // ROWS + 16, channels), BF)
    return call(
        inner_kernel,
        "inner",
        place,
        [grad_rows, third_weight, third_rows, edge],
        [((rows, channels), BF), ((16, channels), BF), rim, rim],
    )


def third_kernel(
    piece, place_ref, left_hbm, right_hbm, weight_hbm,
    keep_ref, send_ref, left_ref, right_ref, weight_ref, sems,
):
    copies = [
        pltpu.make_async_copy(*pair, sems.at[at])
        for at, pair in enumerate(
            ((left_hbm, left_ref), (right_hbm, right_ref), (weight_hbm, weight_ref))
        )
    ]
    for copy in copies:
        copy.start()
    copies[0].wait()
    copies[1].wait()
    channels = left_ref.shape[1]
    step = channels // 4
    for part in range(4):
        term = lax.dot_general(
            left_ref[:, part * step : (part + 1) * step],
            right_ref[...],
            (((0,), (0,)), ((), ())),
            preferred_element_type=F32,
        )
        columns = term.shape[1]
        keep, send = halves(term.reshape(step // (2 * piece), 2, piece, columns), place_ref[0])
        here = slice(part * step // 2, (part + 1) * step // 2)
        keep_ref[here, :] = keep.reshape(step // 2, columns)
        send_ref[here, :] = send.reshape(step // 2, columns).astype(BF)
    copies[2].wait()


def third_of(place, third_rows, grad_rows, third_weight, piece):
    positions, channels = grad_rows.shape
    wide = ((positions, channels), BF)
    return call(
        lambda *refs: third_kernel(piece, *refs),
        "third",
        place,
        [(third_rows,), (grad_rows,), (third_weight,)],
        [
            ((channels // 2, channels), F32),
            ((channels // 2, channels), BF),
            wide,
            wide,
            ((channels, channels), BF),
        ],
        [pltpu.SemaphoreType.DMA((3,))],
    )


def fold_kernel(bit, place_ref, total_ref, received_ref, keep_ref, send_ref):
    for at in range(total_ref.shape[0]):
        total = total_ref[at] + received_ref[at].astype(F32)
        keep, send = halves(total[None], place_ref[bit])
        keep_ref[at] = keep[0]
        send_ref[at] = send[0].astype(BF)


def fold_of(place, total, received, left, bit, piece):
    at = left.index(bit)
    columns = total.shape[-1]
    shape = (1 << at, 2, piece << (len(left) - at - 1), columns)
    out = (shape[0], *shape[2:])
    return call(
        lambda *refs: fold_kernel(bit, *refs),
        "fold",
        place,
        [total.reshape(shape), received.reshape(shape)],
        [(out, F32), (out, BF)],
    )


def summed_up(place, keep, send, order, left, piece):
    received = exchange(send, order[0])
    for bit in order[1:]:
        keep, send = fold_of(place, keep, received, left, bit, piece)
        left = [b for b in left if b != bit]
        received = exchange(send, bit)
    columns = keep.shape[-1]
    return keep.reshape(piece, columns), received.reshape(piece, columns)


def ready_kernel(gw, piece, place_ref, weight_ref, input_ref, spread_ref, keep_ref, send_ref):
    shards, _, _, step = spread_ref.shape
    positions = input_ref.shape[0]
    source = lax.broadcasted_iota(jnp.int32, (gw, step), 0)
    column = lax.broadcasted_iota(jnp.int32, (gw, step), 1) % gw
    chooser = jnp.where(source == column, 1.0, 0.0).astype(BF)
    row_group = lax.broadcasted_iota(jnp.int32, (step, step), 0) // gw
    column_group = lax.broadcasted_iota(jnp.int32, (step, step), 1) // gw
    mine = row_group == column_group
    for shard in range(shards):
        here = slice(shard * step, (shard + 1) * step)
        for tap in range(TAPS):
            copies = lax.dot_general(
                weight_ref[tap * gw : (tap + 1) * gw, here],
                chooser,
                (((0,), (0,)), ((), ())),
                preferred_element_type=F32,
            )
            spread_ref[shard, tap // 3, (tap % 3) * step : (tap % 3 + 1) * step, :] = jnp.where(
                mine, copies, 0.0
            ).astype(BF)
        turned = input_ref[:, here]
        if piece % 16:
            turned = turned.astype(F32)
        turned = turned.T.reshape(step // (2 * piece), 2, piece, positions)
        keep, send = halves(turned, place_ref[0])
        here = slice(shard * step // 2, (shard + 1) * step // 2)
        keep_ref[here, :] = keep.reshape(step // 2, positions).astype(BF)
        send_ref[here, :] = send.reshape(step // 2, positions).astype(BF)


def ready_of(place, group_weight, input_rows, shard, gw, piece):
    positions, channels = input_rows.shape
    turned = ((channels // 2, positions), BF)
    return call(
        lambda *refs: ready_kernel(gw, piece, *refs),
        "ready",
        place,
        [group_weight, input_rows],
        [((channels // shard, 3, 3 * shard, shard), BF), turned, turned],
    )


def shifted(line, left, right):
    wide = line.astype(F32)
    width = wide.shape[0]
    at = lax.broadcasted_iota(jnp.int32, wide.shape, 0)
    return (
        jnp.where(at == width - 1, right, pltpu.roll(wide, width - 1, 0)).astype(BF),
        line,
        jnp.where(at == 0, left, pltpu.roll(wide, 1, 0)).astype(BF),
    )


def own_groups(term, gw):
    step = term.shape[1]
    lane_group = lax.broadcasted_iota(jnp.int32, (gw, step), 1) // gw
    mine = term[:gw]
    for group in range(1, step // gw):
        mine = jnp.where(lane_group == group, term[group * gw : (group + 1) * gw], mine)
    return mine


def body_kernel(
    gw, near, place_ref, inner_ref, edge_ref, own_ref, other_ref, spread_ref,
    back_ref, term_ref, window_ref,
):
    positions = inner_ref.shape[0]
    step = own_ref.shape[2]
    width = positions // ROWS
    core = place_ref[0]
    side = place_ref[1] if near else 1 - place_ref[1]
    for slot, second_ref in enumerate((own_ref, other_ref)):
        shard = 2 * side + (core if slot == 0 else 1 - core)
        columns = pl.ds(pl.multiple_of(shard * step, step), step)
        edges = edge_ref[:, columns].astype(F32)
        for row in range(ROWS):
            here = pl.ds(row * width, width)
            edge = edges[row : row + 1]
            left, right = jnp.where(core == 1, edge, 0.0), jnp.where(core == 0, edge, 0.0)
            for at, line in enumerate(shifted(inner_ref[here, columns], left, right)):
                window_ref[here, at * step : (at + 1) * step] = line
        flipped = second_ref[...].reshape(positions, step).T
        for tap_row in (1, 0, 2):
            count = ROWS if tap_row == 1 else ROWS - 1
            take = pl.ds(width if tap_row == 0 else 0, count * width)
            start = width if tap_row == 2 else 0
            put = pl.ds(start, count * width)
            window = window_ref[take, :]
            back = jnp.dot(window, spread_ref[shard, tap_row], preferred_element_type=F32)
            term = jnp.dot(
                flipped[:, start : start + count * width], window, preferred_element_type=F32
            )
            for tap_col in range(3):
                tap = 3 * tap_row + tap_col
                term_ref[slot, tap * gw : (tap + 1) * gw, :] = own_groups(
                    term[:, tap_col * step : (tap_col + 1) * step], gw
                )
            if tap_row == 1:
                back_ref[slot] = back
            else:
                back_ref[slot, put, :] += back


def body_of(place, near, inner, edge, own, other, spread, gw):
    positions = inner.shape[0]
    shard = own.shape[2]
    return call(
        lambda *refs: body_kernel(gw, near, *refs),
        "body_near" if near else "body_far",
        place,
        [inner, edge, own, other, spread],
        [((2, positions, shard), F32), ((2, TAPS * gw, shard), F32)],
        [pltpu.VMEM((positions, 3 * shard), BF)],
    )


def close_kernel(
    gw, piece, near, place_ref, back_ref, term_ref, own_ref, other_ref, inside_ref, outside_ref,
    spread_ref, keep_in_ref, send_in_ref,
    first_ref, keep_ref, send_ref, group_keep_ref, group_send_ref,
):
    _, positions, step = back_ref.shape
    width = positions // ROWS
    core, half = place_ref[0], place_ref[1]
    side = half if near else 1 - half
    for slot, second_ref in enumerate((own_ref, other_ref)):
        turn = core if slot == 0 else 1 - core
        shard = 2 * side + turn
        columns = pl.ds(pl.multiple_of(shard * step, step), step)
        inside, outside = inside_ref[:, columns], outside_ref[:, columns]
        second = second_ref[...].reshape(positions, step)
        backs, terms = {}, {}
        for tap_row, row in ((2, 0), (0, ROWS - 1)):
            rim = jnp.where(half == (0 if row == 0 else 1), outside, inside)
            edge = rim[width:].astype(F32)[0:1]
            left, right = jnp.where(core == 1, edge, 0.0), jnp.where(core == 0, edge, 0.0)
            flipped = second[row * width : (row + 1) * width].T
            window = jnp.concatenate(shifted(rim[:width], left, right), 1)
            backs[row] = jnp.dot(window, spread_ref[shard, tap_row], preferred_element_type=F32)
            term = jnp.dot(flipped, window, preferred_element_type=F32)
            terms[tap_row] = [
                own_groups(term[:, at * step : (at + 1) * step], gw) for at in range(3)
            ]
        lines = []
        for row in range(ROWS):
            here = slice(row * width, (row + 1) * width)
            back = back_ref[slot, here, :]
            if row in backs:
                back = back + backs[row]
            lines.append(jnp.where(second[here] > 0, back, 0.0).astype(BF))
        first = jnp.concatenate(lines)
        place_at = pl.ds(pl.multiple_of(turn * step, step), step)
        first_ref[:, place_at] = first
        keep_ref[:, place_at] = jnp.dot(keep_in_ref[...], first, preferred_element_type=F32)
        send_ref[:, place_at] = jnp.dot(
            send_in_ref[...], first, preferred_element_type=F32
        ).astype(BF)
        term = term_ref[slot]
        parts = []
        for tap_row in range(3):
            part = term[3 * tap_row * gw : 3 * (tap_row + 1) * gw]
            if tap_row in terms:
                part = part + jnp.concatenate(terms[tap_row])
            parts.append(part)
        turned = jnp.concatenate(parts).T.reshape(step // (2 * piece), 2, piece, TAPS * gw)
        keep, send = halves(turned, core)
        here = pl.ds(pl.multiple_of(turn * (step // 2), step // 2), step // 2)
        group_keep_ref[here, :] = keep.reshape(step // 2, TAPS * gw)
        group_send_ref[here, :] = send.reshape(step // 2, TAPS * gw).astype(BF)


def close_of(place, near, back, term, own, other, inside, outside, spread, keep_in, send_in, piece):
    _, positions, shard = back.shape
    rows = keep_in.shape[0]
    gw = term.shape[1] // TAPS
    return call(
        lambda *refs: close_kernel(gw, piece, near, *refs),
        "close_near" if near else "close_far",
        place,
        [back, term, own, other, inside, outside, spread, keep_in, send_in],
        [
            ((positions, 2 * shard), BF),
            ((rows, 2 * shard), F32),
            ((rows, 2 * shard), BF),
            ((shard, TAPS * gw), F32),
            ((shard, TAPS * gw), BF),
        ],
    )


def split_kernel(
    piece,
    place_ref,
    near_ref,
    far_ref,
    near_got_ref,
    far_got_ref,
    group_near_ref,
    group_far_ref,
    group_near_got_ref,
    group_far_got_ref,
    one_keep_ref,
    one_send_ref,
    two_keep_ref,
    two_send_ref,
):
    half = place_ref[1]
    pre = one_keep_ref.shape[0]
    size = 4 * piece

    def by_second(value):
        keep, send = halves(value.reshape(1, 2, size // 2, value.shape[1]), place_ref[2])
        return keep[0], send[0].astype(BF)

    def by_first(value):
        keep, send = halves(value.reshape(2, 2, piece, value.shape[1]), half)
        rows = (size // 2, value.shape[1])
        return keep.reshape(rows), send.reshape(rows).astype(BF)

    for at in range(pre):
        here = slice(at * size, (at + 1) * size)
        near = near_ref[here, :] + near_got_ref[here, :].astype(F32)
        far = far_ref[here, :] + far_got_ref[here, :].astype(F32)
        low = jnp.where(half == 0, near, far)
        high = jnp.where(half == 0, far, near)
        there = slice(at % (pre // 2) * size, (at % (pre // 2) + 1) * size)
        group = jnp.where(
            half == at // (pre // 2),
            group_near_ref[there, :] + group_near_got_ref[there, :].astype(F32),
            group_far_ref[there, :] + group_far_got_ref[there, :].astype(F32),
        )
        cut = low.shape[1] // 2
        one_keep_ref[at, :, :cut], one_send_ref[at, :, :cut] = by_second(low[:, :cut])
        one_keep_ref[at, :, cut:], one_send_ref[at, :, cut:] = by_second(group)
        two_keep_ref[at, :, :cut], two_send_ref[at, :, :cut] = by_first(low[:, cut:])
        two_keep_ref[at, :, cut:], two_send_ref[at, :, cut:] = by_first(high)


def split_of(place, near, far, near_got, far_got, group, group_got, piece):
    rows, columns = near.shape
    pre = rows // (4 * piece)
    cut = columns // 2
    outs = []
    for size in (cut + group[0].shape[1], cut + columns):
        for kind in (F32, BF):
            outs.append(((pre, 2 * piece, size), kind))
    return call(
        lambda *refs: split_kernel(piece, *refs),
        "split",
        place,
        [near, far, near_got, far_got, *group, *group_got],
        outs,
    )


def last_kernel(scale, place_ref, one_ref, one_got_ref, two_ref, two_got_ref, first_ref, group_ref):
    one = (one_ref[...] + one_got_ref[...].astype(F32)) * scale
    cut = one.shape[1] - group_ref.shape[1]
    first_ref[:, :cut] = one[:, :cut]
    group_ref[...] = one[:, cut:]
    first_ref[:, cut:] = (two_ref[...] + two_got_ref[...].astype(F32)) * scale


def last_of(place, scale, one, one_got, two, two_got, channels, group_columns):
    piece = one.shape[0]
    return call(
        lambda *refs: last_kernel(scale, *refs),
        "last",
        place,
        [one, one_got, two, two_got],
        [((piece, channels), F32), ((piece, group_columns), F32)],
        pinned=False,
    )


def result_kernel(place_ref, near_ref, far_ref, grad_ref, weight_hbm, out_hbm, weight_ref, out_ref, sems):
    channels = grad_ref.shape[1]
    step = channels // 4
    halfway = channels // 2
    pieces = [pl.ds(part * step, step) for part in range(4)]
    copies = [
        pltpu.make_async_copy(weight_hbm.at[here], weight_ref.at[here], sems.at[part])
        for part, here in enumerate(pieces)
    ]
    for copy in copies:
        copy.start()
    near = pl.ds(pl.multiple_of(place_ref[1] * halfway, halfway), halfway)
    far = pl.ds(pl.multiple_of((1 - place_ref[1]) * halfway, halfway), halfway)
    outs = []
    for part, here in enumerate(pieces):
        copies[part].wait()
        summed = nt_dot(near_ref[...], weight_ref[here, near])
        summed += nt_dot(far_ref[...], weight_ref[here, far])
        columns = slice(part * step, (part + 1) * step)
        out_ref[:, columns] = (summed + grad_ref[:, columns].astype(F32)).astype(BF)
        outs.append(pltpu.make_async_copy(out_ref.at[:, here], out_hbm.at[:, here], sems.at[4 + part]))
        outs[-1].start()
    for out in outs:
        out.wait()


def result_of(place, near, far, first_weight, grad_rows):
    rows, channels = grad_rows.shape
    vmem, hbm = (pl.BlockSpec(memory_space=kind) for kind in (pltpu.VMEM, pltpu.HBM))
    return pl.pallas_call(
        result_kernel,
        in_specs=[pl.BlockSpec(memory_space=pltpu.SMEM), vmem, vmem, vmem, hbm],
        out_specs=hbm,
        out_shape=jax.ShapeDtypeStruct((rows, channels), BF),
        scratch_shapes=[
            pltpu.VMEM((channels, channels), BF),
            pltpu.VMEM((rows, channels), BF),
            pltpu.SemaphoreType.DMA((8,)),
        ],
        compiler_params=pltpu.CompilerParams(vmem_limit_bytes=12 * 1024 * 1024),
        cost_estimate=pl.CostEstimate(flops=0, bytes_accessed=0, transcendentals=0),
        name="result",
    )(place, near, far, grad_rows, pltpu.with_memory_space_constraint(first_weight, pltpu.HBM))


def per_device(
    outer_grad, block_input, third_input, second_input, third_weight, group_weight, first_weight
):
    devices = lax.axis_size("space")
    position = lax.axis_index("space")
    n_bits = devices.bit_length() - 1
    place = (position >> jnp.arange(n_bits, dtype=jnp.int32)) & 1
    place = place.astype(jnp.int32)
    _, tile_rows, width, channels = outer_grad.shape
    positions = tile_rows * width
    shard = channels // 4
    gw = group_weight.shape[1] // TAPS
    piece = channels // devices
    normalizer = 1.0 / math.sqrt(positions * devices)
    grad_rows = outer_grad.reshape(positions, channels)
    third_rows = third_input.reshape(positions, channels)
    input_rows = block_input.reshape(positions, channels)
    left = list(range(n_bits - 1, 0, -1))
    z_first = [*range(2, n_bits), 1]
    x_first = [*range(1, n_bits)]

    near_own, near_core, far_sent, edge = pack_of(place, second_input, grad_rows, third_rows)
    edge_got = exchange(edge, 0)
    near_other = exchange(near_core, 0)
    far = exchange(far_sent, 1)

    kept, sent, third_copy, grad_copy, weight_copy = third_of(
        after(place, edge), third_rows, grad_rows, third_weight, piece
    )
    inner, edge, inside, outside = inner_of(
        after(place, sent), grad_copy, weight_copy, third_copy, edge_got
    )
    got = exchange(sent, 0)
    kept, sent = fold_of(after(place, inside), kept, got, left, 2, piece)
    inside = exchange(inside, 1)
    outside = exchange_across(outside)

    spread, keep_in, send_in = ready_of(
        after(place, sent, far), group_weight.T, input_rows, shard, gw, piece
    )
    near = body_of(place, True, inner, edge, near_own, near_other, spread, gw)
    far_own = far[0]
    far_other = exchange(far[1], 0)
    far = body_of(after(place, near[0]), False, inner, edge, far_own, far_other, spread, gw)

    order = [2, 1, *range(3, n_bits)]
    left_after = [b for b in left if b != 2]
    got = exchange(sent, 2)
    kept, sent = fold_of(after(place, far[0], inside, outside), kept, got, left_after, order[1], piece)
    closing = after(place, sent)
    left_after.remove(order[1])
    got = exchange(sent, order[1])
    kept, sent = fold_of(place, kept, got, left_after, order[2], piece)
    splitting = after(place, sent)
    left_after.remove(order[2])

    near_first, near_kept, near_send, group_near_kept, group_near_send = close_of(
        closing, True, *near, near_own, near_other, inside, outside, spread, keep_in, send_in, piece
    )
    near_got = exchange(near_send, 0)
    group_near_got = exchange(group_near_send, 0)
    far_first, far_kept, far_send, group_far_kept, group_far_send = close_of(
        closing, False, *far, far_own, far_other, inside, outside, spread, keep_in, send_in, piece
    )
    far_got = exchange(far_send, 0)
    group_far_got = exchange(group_far_send, 0)

    one_kept, one_sent, two_kept, two_sent = split_of(
        place, near_kept, far_kept, near_got, far_got,
        (group_near_kept, group_far_kept), (group_near_got, group_far_got), piece,
    )
    kept, got = summed_up(place, kept, sent, order[2:], left_after, piece)
    third_wgrad = (kept + got.astype(F32)) * normalizer
    one = summed_up(place, one_kept, one_sent, z_first, [b for b in left if b != 2], piece)
    input_grad = result_of(place, near_first, far_first, first_weight, grad_copy)
    two = summed_up(after(place, input_grad), two_kept, two_sent, x_first, [b for b in left if b != 1], piece)
    first_wgrad, group_wgrad = last_of(place, normalizer, *one, *two, channels, TAPS * gw)
    return (input_grad.reshape(outer_grad.shape), third_wgrad, group_wgrad, first_wgrad)


def solution(mesh):
    tiles = P(("parts", "space"), None, None, None)
    rows = P(("parts", "space"), None)
    return jax.shard_map(
        per_device,
        mesh=mesh,
        in_specs=(tiles, tiles, tiles, tiles, P(), P(), P()),
        out_specs=(tiles, rows, rows, rows),
        check_vma=False,
    )
```

```python
import math

import jax
import jax.numpy as jnp
from jax import lax
from jax.experimental import pallas as pl
from jax.experimental.pallas import tpu as pltpu
from jax.sharding import PartitionSpec as P

BF = jnp.bfloat16
F32 = jnp.float32
TAPS = 9
ROWS = 4


def exchange(array, bit):
    count = lax.axis_size("space")
    return lax.ppermute(array, "space", [(i, i ^ (1 << bit)) for i in range(count)])


def exchange_across(array):
    count = lax.axis_size("space")
    route = []
    for low in range(count):
        high = low + 2
        if low & 2 and high < count:
            route += [(low, high), (high, low)]
    return lax.ppermute(array, "space", route)


def after(value, *others):
    return value if not others else lax.optimization_barrier((value, *others))[0]


def call(kernel, name, place, operands, outs, scratch=(), megabytes=12, pinned=True):
    inputs, specs = [], [pl.BlockSpec(memory_space=pltpu.SMEM)]
    for operand in operands:
        if isinstance(operand, tuple):
            inputs.append(pltpu.with_memory_space_constraint(operand[0], pltpu.HBM))
            specs.append(pl.BlockSpec(memory_space=pltpu.HBM))
        else:
            inputs.append(operand)
            specs.append(pl.BlockSpec(memory_space=pltpu.VMEM))
    kind = pltpu.VMEM if pinned else jax.ShapeDtypeStruct
    return pl.pallas_call(
        kernel,
        in_specs=specs,
        out_specs=[pl.BlockSpec(memory_space=pltpu.VMEM)] * len(outs),
        out_shape=[kind(*out) for out in outs],
        scratch_shapes=scratch,
        compiler_params=pltpu.CompilerParams(vmem_limit_bytes=megabytes * 1024 * 1024),
        cost_estimate=pl.CostEstimate(flops=0, bytes_accessed=0, transcendentals=0),
        name=name,
    )(place, *inputs)


def nt_dot(a, b):
    return lax.dot_general(a, b, (((1,), (1,)), ((), ())), preferred_element_type=F32)


def halves(value, bit):
    low, high = value[:, 0], value[:, 1]
    return jnp.where(bit == 0, low, high), jnp.where(bit == 0, high, low)


def inner_kernel(
    place_ref, grad_ref, weight_ref, mask_ref, edge_ref,
    out_ref, rim_ref, inside_ref, outside_ref,
):
    channels = weight_ref.shape[0]
    step = channels // 2
    width = grad_ref.shape[0] // ROWS
    half = place_ref[1]
    for part in range(2):
        here = slice(part * step, (part + 1) * step)
        weight = weight_ref[here, :]
        back = nt_dot(grad_ref[...], weight)
        inner = jnp.where(mask_ref[:, here] > 0, back, 0.0).astype(BF)
        out_ref[:, here] = inner
        beside = nt_dot(edge_ref[...], weight)
        kept = edge_ref[:, here].astype(F32)
        lines = [
            jnp.where(kept[ROWS + row : ROWS + row + 1] > 0, beside[row : row + 1], 0.0)
            for row in range(ROWS)
        ]
        nothing = [jnp.zeros_like(lines[0])]
        rim_ref[:, here] = jnp.concatenate(lines + nothing * (16 - ROWS)).astype(BF)
        first, last = inner[:width], inner[(ROWS - 1) * width :]
        upper = jnp.concatenate([lines[0]] + nothing * 15).astype(BF)
        lower = jnp.concatenate([lines[-1]] + nothing * 15).astype(BF)
        inside_ref[:width, here] = jnp.where(half == 0, last, first)
        inside_ref[width:, here] = jnp.where(half == 0, lower, upper)
        outside_ref[:width, here] = jnp.where(half == 0, first, last)
        outside_ref[width:, here] = jnp.where(half == 0, upper, lower)


def inner_of(place, grad_rows, third_weight, third_rows, edge):
    rows, channels = grad_rows.shape
    rim = ((rows // ROWS + 16, channels), BF)
    return call(
        inner_kernel,
        "inner",
        place,
        [grad_rows, third_weight, third_rows, edge],
        [((rows, channels), BF), ((16, channels), BF), rim, rim],
    )


def front_kernel(
    piece, place_ref, left_hbm, right_hbm, weight_hbm, second_hbm,
    keep_ref, send_ref, left_ref, right_ref, weight_ref,
    near_own_ref, near_core_ref, far_own_ref, far_core_ref, edge_ref, sems,
):
    rows, width, _ = near_own_ref.shape
    core, half = place_ref[0], place_ref[1]
    copies = [(left_hbm, left_ref), (right_hbm, right_ref)]
    for target, row_at, column_at in (
        (far_own_ref, 1 - half, core),
        (far_core_ref, 1 - half, 1 - core),
        (near_core_ref, half, 1 - core),
        (near_own_ref, half, core),
    ):
        source = second_hbm.at[0, pl.ds(row_at * rows, rows), pl.ds(column_at * width, width)]
        copies.append((source, target))
    copies.append((weight_hbm, weight_ref))
    copies = [pltpu.make_async_copy(*pair, sems.at[at]) for at, pair in enumerate(copies)]
    for copy in copies:
        copy.start()
    copies[0].wait()
    copies[1].wait()
    channels = left_ref.shape[1]
    step = channels // 4
    for part in range(4):
        term = lax.dot_general(
            left_ref[:, part * step : (part + 1) * step],
            right_ref[...],
            (((0,), (0,)), ((), ())),
            preferred_element_type=F32,
        )
        columns = term.shape[1]
        keep, send = halves(term.reshape(step // (2 * piece), 2, piece, columns), core)
        here = slice(part * step // 2, (part + 1) * step // 2)
        keep_ref[here, :] = keep.reshape(step // 2, columns)
        send_ref[here, :] = send.reshape(step // 2, columns).astype(BF)
    lines = []
    for value_ref in (right_ref, left_ref):
        for row in range(ROWS):
            first = value_ref[row * width : row * width + 16, :].astype(F32)[0:1]
            last = value_ref[(row + 1) * width - 16 : (row + 1) * width, :].astype(F32)[15:16]
            lines.append(jnp.where(core == 0, last, first))
    lines += [jnp.zeros_like(lines[0])] * (16 - 2 * ROWS)
    edge_ref[...] = jnp.concatenate(lines).astype(BF)
    for copy in copies[2:]:
        copy.wait()


def front_of(place, third_rows, grad_rows, third_weight, second_input, piece):
    positions, channels = grad_rows.shape
    _, rows, columns, shard = second_input.shape
    wide = ((positions, channels), BF)
    quarter = ((rows // 2, columns // 2, shard), BF)
    return call(
        lambda *refs: front_kernel(piece, *refs),
        "front",
        place,
        [(third_rows,), (grad_rows,), (third_weight,), (second_input,)],
        [
            ((channels // 2, channels), F32),
            ((channels // 2, channels), BF),
            wide,
            wide,
            ((channels, channels), BF),
            *[quarter] * 4,
            ((16, channels), BF),
        ],
        [pltpu.SemaphoreType.DMA((7,))],
    )


def fold_kernel(bit, place_ref, total_ref, received_ref, keep_ref, send_ref):
    for at in range(total_ref.shape[0]):
        total = total_ref[at] + received_ref[at].astype(F32)
        keep, send = halves(total[None], place_ref[bit])
        keep_ref[at] = keep[0]
        send_ref[at] = send[0].astype(BF)


def fold_of(place, total, received, left, bit, piece):
    at = left.index(bit)
    columns = total.shape[-1]
    shape = (1 << at, 2, piece << (len(left) - at - 1), columns)
    out = (shape[0], *shape[2:])
    return call(
        lambda *refs: fold_kernel(bit, *refs),
        "fold",
        place,
        [total.reshape(shape), received.reshape(shape)],
        [(out, F32), (out, BF)],
    )


def summed_up(place, keep, send, order, left, piece, gates={}):
    received = exchange(send, order[0])
    sent = []
    for step, bit in enumerate(order[1:]):
        keep, send = fold_of(
            after(place, *gates.get(step, ())), keep, received, left, bit, piece
        )
        left = [b for b in left if b != bit]
        sent.append(send)
        received = exchange(send, bit)
    columns = keep.shape[-1]
    return keep.reshape(piece, columns), received.reshape(piece, columns), sent


def ready_kernel(gw, piece, place_ref, weight_ref, input_ref, spread_ref, keep_ref, send_ref):
    shards, _, _, step = spread_ref.shape
    positions = input_ref.shape[0]
    source = lax.broadcasted_iota(jnp.int32, (gw, step), 0)
    column = lax.broadcasted_iota(jnp.int32, (gw, step), 1) % gw
    chooser = jnp.where(source == column, 1.0, 0.0).astype(BF)
    row_group = lax.broadcasted_iota(jnp.int32, (step, step), 0) // gw
    column_group = lax.broadcasted_iota(jnp.int32, (step, step), 1) // gw
    mine = row_group == column_group
    for shard in range(shards):
        here = slice(shard * step, (shard + 1) * step)
        for tap in range(TAPS):
            copies = lax.dot_general(
                weight_ref[tap * gw : (tap + 1) * gw, here],
                chooser,
                (((0,), (0,)), ((), ())),
                preferred_element_type=F32,
            )
            spread_ref[shard, tap // 3, (tap % 3) * step : (tap % 3 + 1) * step, :] = jnp.where(
                mine, copies, 0.0
            ).astype(BF)
        turned = input_ref[:, here]
        if piece % 16:
            turned = turned.astype(F32)
        turned = turned.T.reshape(step // (2 * piece), 2, piece, positions)
        keep, send = halves(turned, place_ref[0])
        here = slice(shard * step // 2, (shard + 1) * step // 2)
        keep_ref[here, :] = keep.reshape(step // 2, positions).astype(BF)
        send_ref[here, :] = send.reshape(step // 2, positions).astype(BF)


def ready_of(place, group_weight, input_rows, shard, gw, piece):
    positions, channels = input_rows.shape
    turned = ((channels // 2, positions), BF)
    return call(
        lambda *refs: ready_kernel(gw, piece, *refs),
        "ready",
        place,
        [group_weight, input_rows],
        [((channels // shard, 3, 3 * shard, shard), BF), turned, turned],
    )


def shifted(line, left, right):
    wide = line.astype(F32)
    width = wide.shape[0]
    at = lax.broadcasted_iota(jnp.int32, wide.shape, 0)
    return (
        jnp.where(at == width - 1, right, pltpu.roll(wide, width - 1, 0)).astype(BF),
        line,
        jnp.where(at == 0, left, pltpu.roll(wide, 1, 0)).astype(BF),
    )


def own_groups(term, gw):
    step = term.shape[1]
    lane_group = lax.broadcasted_iota(jnp.int32, (gw, step), 1) // gw
    mine = term[:gw]
    for group in range(1, step // gw):
        mine = jnp.where(lane_group == group, term[group * gw : (group + 1) * gw], mine)
    return mine


def body_kernel(
    gw, near, place_ref, inner_ref, edge_ref, own_ref, other_ref, spread_ref,
    back_ref, term_ref, window_ref,
):
    positions = inner_ref.shape[0]
    step = own_ref.shape[2]
    width = positions // ROWS
    core = place_ref[0]
    side = place_ref[1] if near else 1 - place_ref[1]
    for slot, second_ref in enumerate((own_ref, other_ref)):
        shard = 2 * side + (core if slot == 0 else 1 - core)
        columns = pl.ds(pl.multiple_of(shard * step, step), step)
        edges = edge_ref[:, columns].astype(F32)
        for row in range(ROWS):
            here = pl.ds(row * width, width)
            edge = edges[row : row + 1]
            left, right = jnp.where(core == 1, edge, 0.0), jnp.where(core == 0, edge, 0.0)
            for at, line in enumerate(shifted(inner_ref[here, columns], left, right)):
                window_ref[here, at * step : (at + 1) * step] = line
        flipped = second_ref[...].reshape(positions, step).T
        for tap_row in (1, 0, 2):
            count = ROWS if tap_row == 1 else ROWS - 1
            take = pl.ds(width if tap_row == 0 else 0, count * width)
            start = width if tap_row == 2 else 0
            put = pl.ds(start, count * width)
            window = window_ref[take, :]
            back = jnp.dot(window, spread_ref[shard, tap_row], preferred_element_type=F32)
            term = jnp.dot(
                flipped[:, start : start + count * width], window, preferred_element_type=F32
            )
            for tap_col in range(3):
                tap = 3 * tap_row + tap_col
                term_ref[slot, tap * gw : (tap + 1) * gw, :] = own_groups(
                    term[:, tap_col * step : (tap_col + 1) * step], gw
                )
            if tap_row == 1:
                back_ref[slot] = back
            else:
                back_ref[slot, put, :] += back


def body_of(place, near, inner, edge, own, other, spread, gw):
    positions = inner.shape[0]
    shard = own.shape[2]
    return call(
        lambda *refs: body_kernel(gw, near, *refs),
        "body_near" if near else "body_far",
        place,
        [inner, edge, own, other, spread],
        [((2, positions, shard), F32), ((2, TAPS * gw, shard), F32)],
        [pltpu.VMEM((positions, 3 * shard), BF)],
    )


def close_kernel(
    gw, piece, near, place_ref, back_ref, term_ref, own_ref, other_ref, inside_ref, outside_ref,
    spread_ref, keep_in_ref, send_in_ref,
    first_ref, keep_ref, send_ref, group_keep_ref, group_send_ref,
):
    _, positions, step = back_ref.shape
    width = positions // ROWS
    core, half = place_ref[0], place_ref[1]
    side = half if near else 1 - half
    for slot, second_ref in enumerate((own_ref, other_ref)):
        turn = core if slot == 0 else 1 - core
        shard = 2 * side + turn
        columns = pl.ds(pl.multiple_of(shard * step, step), step)
        inside, outside = inside_ref[:, columns], outside_ref[:, columns]
        second = second_ref[...].reshape(positions, step)
        backs, terms = {}, {}
        for tap_row, row in ((2, 0), (0, ROWS - 1)):
            rim = jnp.where(half == (0 if row == 0 else 1), outside, inside)
            edge = rim[width:].astype(F32)[0:1]
            left, right = jnp.where(core == 1, edge, 0.0), jnp.where(core == 0, edge, 0.0)
            flipped = second[row * width : (row + 1) * width].T
            window = jnp.concatenate(shifted(rim[:width], left, right), 1)
            backs[row] = jnp.dot(window, spread_ref[shard, tap_row], preferred_element_type=F32)
            term = jnp.dot(flipped, window, preferred_element_type=F32)
            terms[tap_row] = [
                own_groups(term[:, at * step : (at + 1) * step], gw) for at in range(3)
            ]
        lines = []
        for row in range(ROWS):
            here = slice(row * width, (row + 1) * width)
            back = back_ref[slot, here, :]
            if row in backs:
                back = back + backs[row]
            lines.append(jnp.where(second[here] > 0, back, 0.0).astype(BF))
        first = jnp.concatenate(lines)
        place_at = pl.ds(pl.multiple_of(turn * step, step), step)
        first_ref[:, place_at] = first
        keep_ref[:, place_at] = jnp.dot(keep_in_ref[...], first, preferred_element_type=F32)
        send_ref[:, place_at] = jnp.dot(
            send_in_ref[...], first, preferred_element_type=F32
        ).astype(BF)
        term = term_ref[slot]
        parts = []
        for tap_row in range(3):
            part = term[3 * tap_row * gw : 3 * (tap_row + 1) * gw]
            if tap_row in terms:
                part = part + jnp.concatenate(terms[tap_row])
            parts.append(part)
        turned = jnp.concatenate(parts).T.reshape(step // (2 * piece), 2, piece, TAPS * gw)
        keep, send = halves(turned, core)
        here = pl.ds(pl.multiple_of(turn * (step // 2), step // 2), step // 2)
        group_keep_ref[here, :] = keep.reshape(step // 2, TAPS * gw)
        group_send_ref[here, :] = send.reshape(step // 2, TAPS * gw).astype(BF)


def close_of(place, near, back, term, own, other, inside, outside, spread, keep_in, send_in, piece):
    _, positions, shard = back.shape
    rows = keep_in.shape[0]
    gw = term.shape[1] // TAPS
    return call(
        lambda *refs: close_kernel(gw, piece, near, *refs),
        "close_near" if near else "close_far",
        place,
        [back, term, own, other, inside, outside, spread, keep_in, send_in],
        [
            ((positions, 2 * shard), BF),
            ((rows, 2 * shard), F32),
            ((rows, 2 * shard), BF),
            ((shard, TAPS * gw), F32),
            ((shard, TAPS * gw), BF),
        ],
    )


def both_halves(half, near_ref, far_ref, near_got_ref, far_got_ref, here):
    near = near_ref[here, :] + near_got_ref[here, :].astype(F32)
    far = far_ref[here, :] + far_got_ref[here, :].astype(F32)
    return jnp.where(half == 0, near, far), jnp.where(half == 0, far, near)


def split_kernel(
    cut, piece, place_ref, near_ref, far_ref, near_got_ref, far_got_ref, keep_ref, send_ref
):
    size = 4 * piece
    for at in range(keep_ref.shape[0]):
        here = slice(at * size, (at + 1) * size)
        low, high = both_halves(
            place_ref[1], near_ref, far_ref, near_got_ref, far_got_ref, here
        )
        edge = low.shape[1] - cut
        for columns, value in ((slice(0, edge), low[:, cut:]), (slice(edge, None), high)):
            keep, send = halves(value.reshape(2, 2, piece, value.shape[1]), place_ref[1])
            rows = (size // 2, value.shape[1])
            keep_ref[at, :, columns] = keep.reshape(rows)
            send_ref[at, :, columns] = send.reshape(rows).astype(BF)


def split_group_kernel(cut, piece, place_ref, *refs):
    *wide, near_ref, far_ref, near_got_ref, far_got_ref, keep_ref, send_ref = refs
    half = place_ref[1]
    pre = keep_ref.shape[0]
    size = 4 * piece
    for at in range(pre):
        there = slice(at % (pre // 2) * size, (at % (pre // 2) + 1) * size)
        value = jnp.where(
            half == at // (pre // 2),
            near_ref[there, :] + near_got_ref[there, :].astype(F32),
            far_ref[there, :] + far_got_ref[there, :].astype(F32),
        )
        parts = [(slice(cut, None), value)]
        if cut:
            low, _ = both_halves(half, *wide, slice(at * size, (at + 1) * size))
            parts.append((slice(0, cut), low[:, :cut]))
        for columns, value in parts:
            keep, send = halves(value.reshape(1, 2, size // 2, value.shape[1]), place_ref[2])
            keep_ref[at, :, columns] = keep[0]
            send_ref[at, :, columns] = send[0].astype(BF)


def split_of(place, near, far, near_got, far_got, cut, piece):
    rows, columns = near.shape
    out = (rows // (4 * piece), 2 * piece, 2 * columns - cut)
    return call(
        lambda *refs: split_kernel(cut, piece, *refs),
        "split",
        place,
        [near, far, near_got, far_got],
        [(out, F32), (out, BF)],
    )


def split_group_of(place, wide, group, cut, piece):
    rows = wide[0].shape[0]
    out = (rows // (4 * piece), 2 * piece, cut + group[0].shape[1])
    return call(
        lambda *refs: split_group_kernel(cut, piece, *refs),
        "split_group",
        place,
        [*(wide if cut else ()), *group],
        [(out, F32), (out, BF)],
    )


def last_kernel(scale, place_ref, one_ref, one_got_ref, two_ref, two_got_ref, first_ref, group_ref):
    one = (one_ref[...] + one_got_ref[...].astype(F32)) * scale
    cut = one.shape[1] - group_ref.shape[1]
    if cut:
        first_ref[:, :cut] = one[:, :cut]
    group_ref[...] = one[:, cut:]
    first_ref[:, cut:] = (two_ref[...] + two_got_ref[...].astype(F32)) * scale


def last_of(place, scale, one, one_got, two, two_got, channels, group_columns):
    piece = one.shape[0]
    return call(
        lambda *refs: last_kernel(scale, *refs),
        "last",
        place,
        [one, one_got, two, two_got],
        [((piece, channels), F32), ((piece, group_columns), F32)],
        pinned=False,
    )


def result_kernel(place_ref, near_ref, far_ref, grad_ref, weight_ref, out_hbm, out_ref, sems):
    channels = grad_ref.shape[1]
    step = channels // 4
    halfway = channels // 2
    near = pl.ds(pl.multiple_of(place_ref[1] * halfway, halfway), halfway)
    far = pl.ds(pl.multiple_of((1 - place_ref[1]) * halfway, halfway), halfway)
    outs = []
    for part in range(4):
        here = slice(part * step, (part + 1) * step)
        summed = nt_dot(near_ref[...], weight_ref[here, near])
        summed += nt_dot(far_ref[...], weight_ref[here, far])
        out_ref[:, here] = (summed + grad_ref[:, here].astype(F32)).astype(BF)
        columns = pl.ds(part * step, step)
        outs.append(
            pltpu.make_async_copy(out_ref.at[:, columns], out_hbm.at[:, columns], sems.at[part])
        )
        outs[-1].start()
    for out in outs:
        out.wait()


def result_of(place, near, far, first_weight, grad_rows):
    rows, channels = grad_rows.shape
    vmem, hbm = (pl.BlockSpec(memory_space=kind) for kind in (pltpu.VMEM, pltpu.HBM))
    return pl.pallas_call(
        result_kernel,
        in_specs=[pl.BlockSpec(memory_space=pltpu.SMEM), vmem, vmem, vmem, vmem],
        out_specs=hbm,
        out_shape=jax.ShapeDtypeStruct((rows, channels), BF),
        scratch_shapes=[pltpu.VMEM((rows, channels), BF), pltpu.SemaphoreType.DMA((4,))],
        compiler_params=pltpu.CompilerParams(vmem_limit_bytes=12 * 1024 * 1024),
        cost_estimate=pl.CostEstimate(flops=0, bytes_accessed=0, transcendentals=0),
        name="result",
    )(place, near, far, grad_rows, first_weight)


def per_device(
    outer_grad, block_input, third_input, second_input, third_weight, group_weight, first_weight
):
    devices = lax.axis_size("space")
    position = lax.axis_index("space")
    n_bits = devices.bit_length() - 1
    place = (position >> jnp.arange(n_bits, dtype=jnp.int32)) & 1
    place = place.astype(jnp.int32)
    _, tile_rows, width, channels = outer_grad.shape
    positions = tile_rows * width
    shard = channels // 4
    gw = group_weight.shape[1] // TAPS
    piece = channels // devices
    normalizer = 1.0 / math.sqrt(positions * devices)
    grad_rows = outer_grad.reshape(positions, channels)
    third_rows = third_input.reshape(positions, channels)
    input_rows = block_input.reshape(positions, channels)
    left = list(range(n_bits - 1, 0, -1))
    z_first = [*range(2, n_bits), 1]
    x_first = [*range(1, n_bits)]

    (
        kept, sent, third_copy, grad_copy, weight_copy,
        near_own, near_core, far_own, far_core, edge,
    ) = front_of(place, third_rows, grad_rows, third_weight, second_input, piece)
    edge_got = exchange(edge, 0)
    near_other = exchange(near_core, 0)
    far_own = exchange(far_own, 1)
    far_core = exchange(far_core, 1)
    got = exchange(sent, 0)

    kept, sent = fold_of(place, kept, got, left, 2, piece)
    inner, edge, inside, outside = inner_of(
        after(place, sent), grad_copy, weight_copy, third_copy, edge_got
    )
    inside = exchange(inside, 1)
    outside = exchange_across(outside)

    spread, keep_in, send_in = ready_of(
        after(place, sent, far_core, far_own), group_weight.T, input_rows, shard, gw, piece
    )
    near = body_of(place, True, inner, edge, near_own, near_other, spread, gw)
    far_other = exchange(far_core, 0)
    far = body_of(after(place, near[0]), False, inner, edge, far_own, far_other, spread, gw)

    order = z_first
    left_after = [b for b in left if b != 2]
    got = exchange(sent, 2)
    kept, sent = fold_of(after(place, far[0], inside, outside), kept, got, left_after, order[1], piece)
    closing = after(place, sent)
    left_after.remove(order[1])
    got = exchange(sent, order[1])
    kept, sent = fold_of(place, kept, got, left_after, order[2], piece)
    splitting = after(place, sent)
    left_after.remove(order[2])

    near_first, near_kept, near_send, group_near_kept, group_near_send = close_of(
        closing, True, *near, near_own, near_other, inside, outside, spread, keep_in, send_in, piece
    )
    near_got = exchange(near_send, 0)
    group_near_got = exchange(group_near_send, 0)
    far_first, far_kept, far_send, group_far_kept, group_far_send = close_of(
        closing, False, *far, far_own, far_other, inside, outside, spread, keep_in, send_in, piece
    )
    far_got = exchange(far_send, 0)
    group_far_got = exchange(group_far_send, 0)

    cut = shard // 2
    wide = (near_kept, far_kept, near_got, far_got)
    two_kept, two_sent = split_of(place, *wide, cut, piece)
    one_kept, one_sent = split_group_of(
        place, wide, (group_near_kept, group_far_kept, group_near_got, group_far_got), cut, piece
    )
    third_sent = sent
    kept, got, _ = summed_up(place, kept, sent, order[2:], left_after, piece)
    third_wgrad = (kept + got.astype(F32)) * normalizer
    input_grad = result_of(place, near_first, far_first, first_weight, grad_copy)
    *two, two_sent = summed_up(
        place, two_kept, two_sent, x_first, [b for b in left if b != 1], piece, {0: (input_grad,)}
    )
    *one, _ = summed_up(
        place, one_kept, one_sent, z_first, [b for b in left if b != 2], piece, {0: (third_sent,), len(z_first) - 2: (two_sent[-1],)}
    )
    first_wgrad, group_wgrad = last_of(place, normalizer, *one, *two, channels, TAPS * gw)
    return (input_grad.reshape(outer_grad.shape), third_wgrad, group_wgrad, first_wgrad)


def solution(mesh):
    tiles = P(("parts", "space"), None, None, None)
    rows = P(("parts", "space"), None)
    return jax.shard_map(
        per_device,
        mesh=mesh,
        in_specs=(tiles, tiles, tiles, tiles, P(), P(), P()),
        out_specs=(tiles, rows, rows, rows),
        check_vma=False,
    )
```

```python
import math

import jax
import jax.numpy as jnp
from jax import lax
from jax.experimental import pallas as pl
from jax.experimental.pallas import tpu as pltpu
from jax.sharding import PartitionSpec as P

BF = jnp.bfloat16
F32 = jnp.float32
TAPS = 9
ROWS = 4


def exchange(array, bit):
    count = lax.axis_size("space")
    return lax.ppermute(array, "space", [(i, i ^ (1 << bit)) for i in range(count)])


def exchange_across(array):
    count = lax.axis_size("space")
    route = []
    for low in range(count):
        high = low + 2
        if low & 2 and high < count:
            route += [(low, high), (high, low)]
    return lax.ppermute(array, "space", route)


def after(value, *others):
    return value if not others else lax.optimization_barrier((value, *others))[0]


def call(kernel, name, place, operands, outs, scratch=(), megabytes=12, pinned=True):
    inputs, specs = [], [pl.BlockSpec(memory_space=pltpu.SMEM)]
    for operand in operands:
        if isinstance(operand, tuple):
            inputs.append(pltpu.with_memory_space_constraint(operand[0], pltpu.HBM))
            specs.append(pl.BlockSpec(memory_space=pltpu.HBM))
        else:
            inputs.append(operand)
            specs.append(pl.BlockSpec(memory_space=pltpu.VMEM))
    kind = pltpu.VMEM if pinned else jax.ShapeDtypeStruct
    return pl.pallas_call(
        kernel,
        in_specs=specs,
        out_specs=[pl.BlockSpec(memory_space=pltpu.VMEM)] * len(outs),
        out_shape=[kind(*out) for out in outs],
        scratch_shapes=scratch,
        compiler_params=pltpu.CompilerParams(vmem_limit_bytes=megabytes * 1024 * 1024),
        cost_estimate=pl.CostEstimate(flops=0, bytes_accessed=0, transcendentals=0),
        name=name,
    )(place, *inputs)


def nt_dot(a, b):
    return lax.dot_general(a, b, (((1,), (1,)), ((), ())), preferred_element_type=F32)


def halves(value, bit):
    low, high = value[:, 0], value[:, 1]
    return jnp.where(bit == 0, low, high), jnp.where(bit == 0, high, low)


def inner_kernel(
    place_ref, grad_ref, weight_ref, mask_ref, edge_ref,
    out_ref, rim_ref, inside_ref, outside_ref,
):
    channels = weight_ref.shape[0]
    step = channels // 2
    width = grad_ref.shape[0] // ROWS
    half = place_ref[1]
    for part in range(2):
        here = slice(part * step, (part + 1) * step)
        weight = weight_ref[here, :]
        back = nt_dot(grad_ref[...], weight)
        inner = jnp.where(mask_ref[:, here] > 0, back, 0.0).astype(BF)
        out_ref[:, here] = inner
        beside = nt_dot(edge_ref[...], weight)
        kept = edge_ref[:, here].astype(F32)
        lines = [
            jnp.where(kept[ROWS + row : ROWS + row + 1] > 0, beside[row : row + 1], 0.0)
            for row in range(ROWS)
        ]
        nothing = [jnp.zeros_like(lines[0])]
        rim_ref[:, here] = jnp.concatenate(lines + nothing * (16 - ROWS)).astype(BF)
        first, last = inner[:width], inner[(ROWS - 1) * width :]
        upper = jnp.concatenate([lines[0]] + nothing * 15).astype(BF)
        lower = jnp.concatenate([lines[-1]] + nothing * 15).astype(BF)
        inside_ref[:width, here] = jnp.where(half == 0, last, first)
        inside_ref[width:, here] = jnp.where(half == 0, lower, upper)
        outside_ref[:width, here] = jnp.where(half == 0, first, last)
        outside_ref[width:, here] = jnp.where(half == 0, upper, lower)


def inner_of(place, grad_rows, third_weight, third_rows, edge):
    rows, channels = grad_rows.shape
    rim = ((rows // ROWS + 16, channels), BF)
    return call(
        inner_kernel,
        "inner",
        place,
        [grad_rows, third_weight, third_rows, edge],
        [((rows, channels), BF), ((16, channels), BF), rim, rim],
    )


def front_kernel(
    piece, place_ref, left_hbm, right_hbm, weight_hbm, second_hbm,
    keep_ref, send_ref, left_ref, right_ref, weight_ref,
    near_own_ref, near_core_ref, far_ref, edge_ref, sems,
):
    rows, width, _ = near_own_ref.shape
    core, half = place_ref[0], place_ref[1]
    copies = [(left_hbm, left_ref), (right_hbm, right_ref)]
    for target, row_at, column_at in (
        (far_ref.at[0], 1 - half, core),
        (far_ref.at[1], 1 - half, 1 - core),
        (near_core_ref, half, 1 - core),
        (near_own_ref, half, core),
    ):
        source = second_hbm.at[0, pl.ds(row_at * rows, rows), pl.ds(column_at * width, width)]
        copies.append((source, target))
    copies.append((weight_hbm, weight_ref))
    copies = [pltpu.make_async_copy(*pair, sems.at[at]) for at, pair in enumerate(copies)]
    for copy in copies:
        copy.start()
    copies[0].wait()
    copies[1].wait()
    channels = left_ref.shape[1]
    step = channels // 4
    for part in range(4):
        term = lax.dot_general(
            left_ref[:, part * step : (part + 1) * step],
            right_ref[...],
            (((0,), (0,)), ((), ())),
            preferred_element_type=F32,
        )
        columns = term.shape[1]
        keep, send = halves(term.reshape(step // (2 * piece), 2, piece, columns), core)
        here = slice(part * step // 2, (part + 1) * step // 2)
        keep_ref[here, :] = keep.reshape(step // 2, columns)
        send_ref[here, :] = send.reshape(step // 2, columns).astype(BF)
    lines = []
    for value_ref in (right_ref, left_ref):
        for row in range(ROWS):
            first = value_ref[row * width : row * width + 16, :].astype(F32)[0:1]
            last = value_ref[(row + 1) * width - 16 : (row + 1) * width, :].astype(F32)[15:16]
            lines.append(jnp.where(core == 0, last, first))
    lines += [jnp.zeros_like(lines[0])] * (16 - 2 * ROWS)
    edge_ref[...] = jnp.concatenate(lines).astype(BF)
    for copy in copies[2:]:
        copy.wait()


def front_of(place, third_rows, grad_rows, third_weight, second_input, piece):
    positions, channels = grad_rows.shape
    _, rows, columns, shard = second_input.shape
    wide = ((positions, channels), BF)
    quarter = (rows // 2, columns // 2, shard)
    return call(
        lambda *refs: front_kernel(piece, *refs),
        "front",
        place,
        [(third_rows,), (grad_rows,), (third_weight,), (second_input,)],
        [
            ((channels // 2, channels), F32),
            ((channels // 2, channels), BF),
            wide,
            wide,
            ((channels, channels), BF),
            (quarter, BF),
            (quarter, BF),
            ((2, *quarter), BF),
            ((16, channels), BF),
        ],
        [pltpu.SemaphoreType.DMA((7,))],
    )


def fold_kernel(bit, got, place_ref, total_ref, *refs):
    received_refs, (keep_ref, *send_refs) = refs[:got], refs[got:]
    pre = total_ref.shape[0]
    for at in range(pre):
        pair = []
        for side in range(2):
            which, row = divmod(2 * at + side, 2 * pre // got)
            pair.append(total_ref[at, side] + received_refs[which][row].astype(F32))
        low, high = pair
        keep_ref[at] = jnp.where(place_ref[bit] == 0, low, high)
        which, row = divmod(at, pre // len(send_refs))
        send_refs[which][row] = jnp.where(place_ref[bit] == 0, high, low).astype(BF)


def fold_of(place, total, received, left, bit, piece, parts=1):
    at = left.index(bit)
    columns = total.shape[-1]
    pre, rows = 1 << at, piece << (len(left) - at - 1)
    got = len(received)
    received = [part.reshape(2 * pre // got, rows, columns) for part in received]
    keep, *send = call(
        lambda *refs: fold_kernel(bit, got, *refs),
        "fold",
        place,
        [total.reshape(pre, 2, rows, columns), *received],
        [((pre, rows, columns), F32)] + [((pre // parts, rows, columns), BF)] * parts,
    )
    return keep, (send if parts > 1 else send[0])


def summed_up(place, keep, send, order, left, piece, gates={}):
    received = exchange(send, order[0])
    sent = []
    for step, bit in enumerate(order[1:]):
        keep, send = fold_of(
            after(place, *gates.get(step, ())), keep, [received], left, bit, piece
        )
        left = [b for b in left if b != bit]
        sent.append(send)
        received = exchange(send, bit)
    columns = keep.shape[-1]
    return keep.reshape(piece, columns), received.reshape(piece, columns), sent


def ready_kernel(gw, piece, place_ref, weight_ref, input_ref, spread_ref, keep_ref, send_ref):
    shards, _, _, step = spread_ref.shape
    positions = input_ref.shape[0]
    source = lax.broadcasted_iota(jnp.int32, (gw, step), 0)
    column = lax.broadcasted_iota(jnp.int32, (gw, step), 1) % gw
    chooser = jnp.where(source == column, 1.0, 0.0).astype(BF)
    row_group = lax.broadcasted_iota(jnp.int32, (step, step), 0) // gw
    column_group = lax.broadcasted_iota(jnp.int32, (step, step), 1) // gw
    mine = row_group == column_group
    for shard in range(shards):
        here = slice(shard * step, (shard + 1) * step)
        for tap in range(TAPS):
            copies = lax.dot_general(
                weight_ref[tap * gw : (tap + 1) * gw, here],
                chooser,
                (((0,), (0,)), ((), ())),
                preferred_element_type=F32,
            )
            spread_ref[shard, tap // 3, (tap % 3) * step : (tap % 3 + 1) * step, :] = jnp.where(
                mine, copies, 0.0
            ).astype(BF)
        turned = input_ref[:, here]
        if piece % 16:
            turned = turned.astype(F32)
        turned = turned.T.reshape(step // (2 * piece), 2, piece, positions)
        keep, send = halves(turned, place_ref[0])
        here = slice(shard * step // 2, (shard + 1) * step // 2)
        keep_ref[here, :] = keep.reshape(step // 2, positions).astype(BF)
        send_ref[here, :] = send.reshape(step // 2, positions).astype(BF)


def ready_of(place, group_weight, input_rows, shard, gw, piece):
    positions, channels = input_rows.shape
    turned = ((channels // 2, positions), BF)
    return call(
        lambda *refs: ready_kernel(gw, piece, *refs),
        "ready",
        place,
        [group_weight, input_rows],
        [((channels // shard, 3, 3 * shard, shard), BF), turned, turned],
    )


def shifted(line, left, right):
    wide = line.astype(F32)
    width = wide.shape[0]
    at = lax.broadcasted_iota(jnp.int32, wide.shape, 0)
    return (
        jnp.where(at == width - 1, right, pltpu.roll(wide, width - 1, 0)).astype(BF),
        line,
        jnp.where(at == 0, left, pltpu.roll(wide, 1, 0)).astype(BF),
    )


def own_groups(term, gw):
    step = term.shape[1]
    lane_group = lax.broadcasted_iota(jnp.int32, (gw, step), 1) // gw
    mine = term[:gw]
    for group in range(1, step // gw):
        mine = jnp.where(lane_group == group, term[group * gw : (group + 1) * gw], mine)
    return mine


def whole(refs, positions, step):
    return jnp.concatenate([ref[...].reshape(-1, step) for ref in refs])


def body_kernel(
    gw, near, place_ref, inner_ref, edge_ref, spread_ref, *refs
):
    *slots, back_ref, term_ref, window_ref = refs
    slots = slots[:1], slots[1:]
    positions, step = back_ref.shape[1:]
    width = positions // ROWS
    core = place_ref[0]
    side = place_ref[1] if near else 1 - place_ref[1]
    for slot, second_refs in enumerate(slots):
        shard = 2 * side + (core if slot == 0 else 1 - core)
        columns = pl.ds(pl.multiple_of(shard * step, step), step)
        edges = edge_ref[:, columns].astype(F32)
        for row in range(ROWS):
            here = pl.ds(row * width, width)
            edge = edges[row : row + 1]
            left, right = jnp.where(core == 1, edge, 0.0), jnp.where(core == 0, edge, 0.0)
            for at, line in enumerate(shifted(inner_ref[here, columns], left, right)):
                window_ref[here, at * step : (at + 1) * step] = line
        flipped = whole(second_refs, positions, step).T
        for tap_row in (1, 0, 2):
            count = ROWS if tap_row == 1 else ROWS - 1
            take = pl.ds(width if tap_row == 0 else 0, count * width)
            start = width if tap_row == 2 else 0
            put = pl.ds(start, count * width)
            window = window_ref[take, :]
            back = jnp.dot(window, spread_ref[shard, tap_row], preferred_element_type=F32)
            term = jnp.dot(
                flipped[:, start : start + count * width], window, preferred_element_type=F32
            )
            for tap_col in range(3):
                tap = 3 * tap_row + tap_col
                term_ref[slot, tap * gw : (tap + 1) * gw, :] = own_groups(
                    term[:, tap_col * step : (tap_col + 1) * step], gw
                )
            if tap_row == 1:
                back_ref[slot] = back
            else:
                back_ref[slot, put, :] += back


def body_of(place, near, inner, edge, own, other, spread, gw):
    positions = inner.shape[0]
    shard = own.shape[2]
    return call(
        lambda *refs: body_kernel(gw, near, *refs),
        "body_near" if near else "body_far",
        place,
        [inner, edge, spread, own, *other],
        [((2, positions, shard), F32), ((2, TAPS * gw, shard), F32)],
        [pltpu.VMEM((positions, 3 * shard), BF)],
    )


def close_kernel(
    gw, piece, near, place_ref, back_ref, term_ref, inside_ref, outside_ref,
    spread_ref, keep_in_ref, send_in_ref, *refs
):
    *slots, first_ref, keep_ref, send_ref, group_keep_ref, group_send_ref = refs
    slots = slots[:1], slots[1:]
    _, positions, step = back_ref.shape
    width = positions // ROWS
    core, half = place_ref[0], place_ref[1]
    side = half if near else 1 - half
    for slot, second_refs in enumerate(slots):
        turn = core if slot == 0 else 1 - core
        shard = 2 * side + turn
        columns = pl.ds(pl.multiple_of(shard * step, step), step)
        inside, outside = inside_ref[:, columns], outside_ref[:, columns]
        second = whole(second_refs, positions, step)
        backs, terms = {}, {}
        for tap_row, row in ((2, 0), (0, ROWS - 1)):
            rim = jnp.where(half == (0 if row == 0 else 1), outside, inside)
            edge = rim[width:].astype(F32)[0:1]
            left, right = jnp.where(core == 1, edge, 0.0), jnp.where(core == 0, edge, 0.0)
            flipped = second[row * width : (row + 1) * width].T
            window = jnp.concatenate(shifted(rim[:width], left, right), 1)
            backs[row] = jnp.dot(window, spread_ref[shard, tap_row], preferred_element_type=F32)
            term = jnp.dot(flipped, window, preferred_element_type=F32)
            terms[tap_row] = [
                own_groups(term[:, at * step : (at + 1) * step], gw) for at in range(3)
            ]
        lines = []
        for row in range(ROWS):
            here = slice(row * width, (row + 1) * width)
            back = back_ref[slot, here, :]
            if row in backs:
                back = back + backs[row]
            lines.append(jnp.where(second[here] > 0, back, 0.0).astype(BF))
        first = jnp.concatenate(lines)
        place_at = pl.ds(pl.multiple_of(turn * step, step), step)
        first_ref[:, place_at] = first
        keep_ref[:, place_at] = jnp.dot(keep_in_ref[...], first, preferred_element_type=F32)
        send_ref[:, place_at] = jnp.dot(
            send_in_ref[...], first, preferred_element_type=F32
        ).astype(BF)
        term = term_ref[slot]
        parts = []
        for tap_row in range(3):
            part = term[3 * tap_row * gw : 3 * (tap_row + 1) * gw]
            if tap_row in terms:
                part = part + jnp.concatenate(terms[tap_row])
            parts.append(part)
        turned = jnp.concatenate(parts).T.reshape(step // (2 * piece), 2, piece, TAPS * gw)
        keep, send = halves(turned, core)
        here = pl.ds(pl.multiple_of(turn * (step // 2), step // 2), step // 2)
        group_keep_ref[here, :] = keep.reshape(step // 2, TAPS * gw)
        group_send_ref[here, :] = send.reshape(step // 2, TAPS * gw).astype(BF)


def close_of(place, near, back, term, own, other, inside, outside, spread, keep_in, send_in, piece):
    _, positions, shard = back.shape
    rows = keep_in.shape[0]
    gw = term.shape[1] // TAPS
    return call(
        lambda *refs: close_kernel(gw, piece, near, *refs),
        "close_near" if near else "close_far",
        place,
        [back, term, inside, outside, spread, keep_in, send_in, own, *other],
        [
            ((positions, 2 * shard), BF),
            ((rows, 2 * shard), F32),
            ((rows, 2 * shard), BF),
            ((shard, TAPS * gw), F32),
            ((shard, TAPS * gw), BF),
        ],
    )


def both_halves(half, near_ref, far_ref, near_got_ref, far_got_ref, here):
    near = near_ref[here, :] + near_got_ref[here, :].astype(F32)
    far = far_ref[here, :] + far_got_ref[here, :].astype(F32)
    return jnp.where(half == 0, near, far), jnp.where(half == 0, far, near)


def split_kernel(
    cut, piece, place_ref, near_ref, far_ref, near_got_ref, far_got_ref, keep_ref, send_ref
):
    size = 4 * piece
    for at in range(keep_ref.shape[0]):
        here = slice(at * size, (at + 1) * size)
        low, high = both_halves(
            place_ref[1], near_ref, far_ref, near_got_ref, far_got_ref, here
        )
        edge = low.shape[1] - cut
        for columns, value in ((slice(0, edge), low[:, cut:]), (slice(edge, None), high)):
            keep, send = halves(value.reshape(2, 2, piece, value.shape[1]), place_ref[1])
            rows = (size // 2, value.shape[1])
            keep_ref[at, :, columns] = keep.reshape(rows)
            send_ref[at, :, columns] = send.reshape(rows).astype(BF)


def split_group_kernel(cut, piece, place_ref, *refs):
    *wide, near_ref, far_ref, near_got_ref, far_got_ref, keep_ref, send_ref = refs
    half = place_ref[1]
    pre = keep_ref.shape[0]
    size = 4 * piece
    for at in range(pre):
        there = slice(at % (pre // 2) * size, (at % (pre // 2) + 1) * size)
        value = jnp.where(
            half == at // (pre // 2),
            near_ref[there, :] + near_got_ref[there, :].astype(F32),
            far_ref[there, :] + far_got_ref[there, :].astype(F32),
        )
        parts = [(slice(cut, None), value)]
        if cut:
            low, _ = both_halves(half, *wide, slice(at * size, (at + 1) * size))
            parts.append((slice(0, cut), low[:, :cut]))
        for columns, value in parts:
            keep, send = halves(value.reshape(1, 2, size // 2, value.shape[1]), place_ref[2])
            keep_ref[at, :, columns] = keep[0]
            send_ref[at, :, columns] = send[0].astype(BF)


def split_of(place, near, far, near_got, far_got, cut, piece):
    rows, columns = near.shape
    out = (rows // (4 * piece), 2 * piece, 2 * columns - cut)
    return call(
        lambda *refs: split_kernel(cut, piece, *refs),
        "split",
        place,
        [near, far, near_got, far_got],
        [(out, F32), (out, BF)],
    )


def split_group_of(place, wide, group, cut, piece):
    rows = wide[0].shape[0]
    out = (rows // (4 * piece), 2 * piece, cut + group[0].shape[1])
    return call(
        lambda *refs: split_group_kernel(cut, piece, *refs),
        "split_group",
        place,
        [*(wide if cut else ()), *group],
        [(out, F32), (out, BF)],
    )


def last_kernel(scale, place_ref, one_ref, one_got_ref, two_ref, two_got_ref, first_ref, group_ref):
    one = (one_ref[...] + one_got_ref[...].astype(F32)) * scale
    cut = one.shape[1] - group_ref.shape[1]
    if cut:
        first_ref[:, :cut] = one[:, :cut]
    group_ref[...] = one[:, cut:]
    first_ref[:, cut:] = (two_ref[...] + two_got_ref[...].astype(F32)) * scale


def last_of(place, scale, one, one_got, two, two_got, channels, group_columns):
    piece = one.shape[0]
    return call(
        lambda *refs: last_kernel(scale, *refs),
        "last",
        place,
        [one, one_got, two, two_got],
        [((piece, channels), F32), ((piece, group_columns), F32)],
        pinned=False,
    )


def result_kernel(place_ref, near_ref, far_ref, grad_ref, weight_ref, out_hbm, out_ref, sems):
    channels = grad_ref.shape[1]
    step = channels // 4
    halfway = channels // 2
    near = pl.ds(pl.multiple_of(place_ref[1] * halfway, halfway), halfway)
    far = pl.ds(pl.multiple_of((1 - place_ref[1]) * halfway, halfway), halfway)
    outs = []
    for part in range(4):
        here = slice(part * step, (part + 1) * step)
        summed = nt_dot(near_ref[...], weight_ref[here, near])
        summed += nt_dot(far_ref[...], weight_ref[here, far])
        out_ref[:, here] = (summed + grad_ref[:, here].astype(F32)).astype(BF)
        columns = pl.ds(part * step, step)
        outs.append(
            pltpu.make_async_copy(out_ref.at[:, columns], out_hbm.at[:, columns], sems.at[part])
        )
        outs[-1].start()
    for out in outs:
        out.wait()


def result_of(place, near, far, first_weight, grad_rows):
    rows, channels = grad_rows.shape
    vmem, hbm = (pl.BlockSpec(memory_space=kind) for kind in (pltpu.VMEM, pltpu.HBM))
    return pl.pallas_call(
        result_kernel,
        in_specs=[pl.BlockSpec(memory_space=pltpu.SMEM), vmem, vmem, vmem, vmem],
        out_specs=hbm,
        out_shape=jax.ShapeDtypeStruct((rows, channels), BF),
        scratch_shapes=[pltpu.VMEM((rows, channels), BF), pltpu.SemaphoreType.DMA((4,))],
        compiler_params=pltpu.CompilerParams(vmem_limit_bytes=12 * 1024 * 1024),
        cost_estimate=pl.CostEstimate(flops=0, bytes_accessed=0, transcendentals=0),
        name="result",
    )(place, near, far, grad_rows, first_weight)


def per_device(
    outer_grad, block_input, third_input, second_input, third_weight, group_weight, first_weight
):
    devices = lax.axis_size("space")
    position = lax.axis_index("space")
    n_bits = devices.bit_length() - 1
    place = (position >> jnp.arange(n_bits, dtype=jnp.int32)) & 1
    place = place.astype(jnp.int32)
    _, tile_rows, width, channels = outer_grad.shape
    positions = tile_rows * width
    shard = channels // 4
    gw = group_weight.shape[1] // TAPS
    piece = channels // devices
    normalizer = 1.0 / math.sqrt(positions * devices)
    grad_rows = outer_grad.reshape(positions, channels)
    third_rows = third_input.reshape(positions, channels)
    input_rows = block_input.reshape(positions, channels)
    left = list(range(n_bits - 1, 0, -1))
    z_first = [*range(2, n_bits), 1]
    x_first = [*range(1, n_bits)]

    (
        kept, sent, third_copy, grad_copy, weight_copy,
        near_own, near_core, far, edge,
    ) = front_of(place, third_rows, grad_rows, third_weight, second_input, piece)
    edge_got = exchange(edge, 0)
    near_other = exchange(near_core, 0)
    far = exchange(far, 1)
    got = exchange(sent, 0)

    kept, sent_parts = fold_of(place, kept, [got], left, 2, piece, parts=2)
    sent = sent_parts[0]
    inner, edge, inside, outside = inner_of(
        after(place, sent), grad_copy, weight_copy, third_copy, edge_got
    )
    inside = exchange(inside, 1)
    outside = exchange_across(outside)

    spread, keep_in, send_in = ready_of(
        after(place, sent), group_weight.T, input_rows, shard, gw, piece
    )
    near = body_of(place, True, inner, edge, near_own, (near_other,), spread, gw)
    far_own = far[0]
    far_other = tuple(exchange(far[1, r : r + ROWS // 2], 0) for r in (0, ROWS // 2))
    far = body_of(after(place, near[0]), False, inner, edge, far_own, far_other, spread, gw)

    order = z_first
    left_after = [b for b in left if b != 2]
    got = [exchange(part, 2) for part in sent_parts]
    kept, sent = fold_of(after(place, near[0]), kept, got, left_after, order[1], piece)
    closing = place
    left_after.remove(order[1])
    got = exchange(sent, order[1])
    kept, sent = fold_of(place, kept, [got], left_after, order[2], piece)
    splitting = after(place, sent)
    left_after.remove(order[2])

    near_first, near_kept, near_send, group_near_kept, group_near_send = close_of(
        closing, True, *near, near_own, (near_other,), inside, outside, spread, keep_in, send_in, piece
    )
    near_got = exchange(after(near_send, sent), 0)
    group_near_got = exchange(group_near_send, 0)
    far_first, far_kept, far_send, group_far_kept, group_far_send = close_of(
        closing, False, *far, far_own, far_other, inside, outside, spread, keep_in, send_in, piece
    )
    far_got = exchange(far_send, 0)
    group_far_got = exchange(group_far_send, 0)

    cut = shard // 2
    wide = (near_kept, far_kept, near_got, far_got)
    two_kept, two_sent = split_of(place, *wide, cut, piece)
    one_kept, one_sent = split_group_of(
        place, wide, (group_near_kept, group_far_kept, group_near_got, group_far_got), cut, piece
    )
    third_sent = sent
    kept, got, _ = summed_up(place, kept, sent, order[2:], left_after, piece)
    third_wgrad = (kept + got.astype(F32)) * normalizer
    input_grad = result_of(place, near_first, far_first, first_weight, grad_copy)
    *two, two_sent = summed_up(
        place, two_kept, two_sent, x_first, [b for b in left if b != 1], piece, {0: (input_grad,)}
    )
    *one, _ = summed_up(
        place, one_kept, one_sent, z_first, [b for b in left if b != 2], piece, {len(z_first) - 2: (two_sent[-1],)}
    )
    first_wgrad, group_wgrad = last_of(place, normalizer, *one, *two, channels, TAPS * gw)
    return (input_grad.reshape(outer_grad.shape), third_wgrad, group_wgrad, first_wgrad)


def solution(mesh):
    tiles = P(("parts", "space"), None, None, None)
    rows = P(("parts", "space"), None)
    return jax.shard_map(
        per_device,
        mesh=mesh,
        in_specs=(tiles, tiles, tiles, tiles, P(), P(), P()),
        out_specs=(tiles, rows, rows, rows),
        check_vma=False,
    )
```

```python
import math

import jax
import jax.numpy as jnp
from jax import lax
from jax.experimental import pallas as pl
from jax.experimental.pallas import tpu as pltpu
from jax.sharding import PartitionSpec as P

BF = jnp.bfloat16
F32 = jnp.float32
TAPS = 9
ROWS = 4


def exchange(array, bit):
    count = lax.axis_size("space")
    return lax.ppermute(array, "space", [(i, i ^ (1 << bit)) for i in range(count)])


def exchange_across(array):
    count = lax.axis_size("space")
    route = []
    for low in range(count):
        high = low + 2
        if low & 2 and high < count:
            route += [(low, high), (high, low)]
    return lax.ppermute(array, "space", route)


def after(value, *others):
    return value if not others else lax.optimization_barrier((value, *others))[0]


def call(kernel, name, place, operands, outs, scratch=(), megabytes=12, pinned=True):
    inputs, specs = [], [pl.BlockSpec(memory_space=pltpu.SMEM)]
    for operand in operands:
        if isinstance(operand, tuple):
            inputs.append(pltpu.with_memory_space_constraint(operand[0], pltpu.HBM))
            specs.append(pl.BlockSpec(memory_space=pltpu.HBM))
        else:
            inputs.append(operand)
            specs.append(pl.BlockSpec(memory_space=pltpu.VMEM))
    kind = pltpu.VMEM if pinned else jax.ShapeDtypeStruct
    return pl.pallas_call(
        kernel,
        in_specs=specs,
        out_specs=[pl.BlockSpec(memory_space=pltpu.VMEM)] * len(outs),
        out_shape=[kind(*out) for out in outs],
        scratch_shapes=scratch,
        compiler_params=pltpu.CompilerParams(vmem_limit_bytes=megabytes * 1024 * 1024),
        cost_estimate=pl.CostEstimate(flops=0, bytes_accessed=0, transcendentals=0),
        name=name,
    )(place, *inputs)


def nt_dot(a, b):
    return lax.dot_general(a, b, (((1,), (1,)), ((), ())), preferred_element_type=F32)


def halves(value, bit):
    low, high = value[:, 0], value[:, 1]
    return jnp.where(bit == 0, low, high), jnp.where(bit == 0, high, low)


def inner_kernel(
    place_ref, grad_ref, weight_ref, mask_ref, edge_ref,
    out_ref, rim_ref, inside_ref, outside_ref,
):
    channels = weight_ref.shape[0]
    step = channels // 2
    width = grad_ref.shape[0] // ROWS
    half = place_ref[1]
    for part in range(2):
        here = slice(part * step, (part + 1) * step)
        weight = weight_ref[here, :]
        back = nt_dot(grad_ref[...], weight)
        inner = jnp.where(mask_ref[:, here] > 0, back, 0.0).astype(BF)
        out_ref[:, here] = inner
        beside = nt_dot(edge_ref[...], weight)
        kept = edge_ref[:, here].astype(F32)
        lines = [
            jnp.where(kept[ROWS + row : ROWS + row + 1] > 0, beside[row : row + 1], 0.0)
            for row in range(ROWS)
        ]
        nothing = [jnp.zeros_like(lines[0])]
        rim_ref[:, here] = jnp.concatenate(lines + nothing * (16 - ROWS)).astype(BF)
        first, last = inner[:width], inner[(ROWS - 1) * width :]
        upper = jnp.concatenate([lines[0]] + nothing * 15).astype(BF)
        lower = jnp.concatenate([lines[-1]] + nothing * 15).astype(BF)
        inside_ref[:width, here] = jnp.where(half == 0, last, first)
        inside_ref[width:, here] = jnp.where(half == 0, lower, upper)
        outside_ref[:width, here] = jnp.where(half == 0, first, last)
        outside_ref[width:, here] = jnp.where(half == 0, upper, lower)


def inner_of(place, grad_rows, third_weight, third_rows, edge):
    rows, channels = grad_rows.shape
    rim = ((rows // ROWS + 16, channels), BF)
    return call(
        inner_kernel,
        "inner",
        place,
        [grad_rows, third_weight, third_rows, edge],
        [((rows, channels), BF), ((16, channels), BF), rim, rim],
    )


def front_kernel(
    piece, place_ref, left_hbm, right_hbm, weight_hbm, second_hbm,
    keep_ref, send_ref, left_ref, right_ref, weight_ref,
    near_own_ref, near_core_ref, far_ref, edge_ref, sems,
):
    rows, width, _ = near_own_ref.shape
    core, half = place_ref[0], place_ref[1]
    copies = [(left_hbm, left_ref), (right_hbm, right_ref)]
    for target, row_at, column_at in (
        (far_ref.at[0], 1 - half, core),
        (far_ref.at[1], 1 - half, 1 - core),
        (near_core_ref, half, 1 - core),
        (near_own_ref, half, core),
    ):
        source = second_hbm.at[0, pl.ds(row_at * rows, rows), pl.ds(column_at * width, width)]
        copies.append((source, target))
    copies.append((weight_hbm, weight_ref))
    copies = [pltpu.make_async_copy(*pair, sems.at[at]) for at, pair in enumerate(copies)]
    for copy in copies:
        copy.start()
    copies[0].wait()
    copies[1].wait()
    channels = left_ref.shape[1]
    step = channels // 4
    for part in range(4):
        term = lax.dot_general(
            left_ref[:, part * step : (part + 1) * step],
            right_ref[...],
            (((0,), (0,)), ((), ())),
            preferred_element_type=F32,
        )
        columns = term.shape[1]
        keep, send = halves(term.reshape(step // (2 * piece), 2, piece, columns), core)
        here = slice(part * step // 2, (part + 1) * step // 2)
        keep_ref[here, :] = keep.reshape(step // 2, columns)
        send_ref[here, :] = send.reshape(step // 2, columns).astype(BF)
    lines = []
    for value_ref in (right_ref, left_ref):
        for row in range(ROWS):
            first = value_ref[row * width : row * width + 16, :].astype(F32)[0:1]
            last = value_ref[(row + 1) * width - 16 : (row + 1) * width, :].astype(F32)[15:16]
            lines.append(jnp.where(core == 0, last, first))
    lines += [jnp.zeros_like(lines[0])] * (16 - 2 * ROWS)
    edge_ref[...] = jnp.concatenate(lines).astype(BF)
    for copy in copies[2:]:
        copy.wait()


def front_of(place, third_rows, grad_rows, third_weight, second_input, piece):
    positions, channels = grad_rows.shape
    _, rows, columns, shard = second_input.shape
    wide = ((positions, channels), BF)
    quarter = (rows // 2, columns // 2, shard)
    return call(
        lambda *refs: front_kernel(piece, *refs),
        "front",
        place,
        [(third_rows,), (grad_rows,), (third_weight,), (second_input,)],
        [
            ((channels // 2, channels), F32),
            ((channels // 2, channels), BF),
            wide,
            wide,
            ((channels, channels), BF),
            (quarter, BF),
            (quarter, BF),
            ((2, *quarter), BF),
            ((16, channels), BF),
        ],
        [pltpu.SemaphoreType.DMA((7,))],
    )


def fold_kernel(bit, got, place_ref, total_ref, *refs):
    received_refs, (keep_ref, *send_refs) = refs[:got], refs[got:]
    pre = total_ref.shape[0]
    for at in range(pre):
        pair = []
        for side in range(2):
            which, row = divmod(2 * at + side, 2 * pre // got)
            pair.append(total_ref[at, side] + received_refs[which][row].astype(F32))
        low, high = pair
        keep_ref[at] = jnp.where(place_ref[bit] == 0, low, high)
        which, row = divmod(at, pre // len(send_refs))
        send_refs[which][row] = jnp.where(place_ref[bit] == 0, high, low).astype(BF)


def fold_of(place, total, received, left, bit, piece, parts=1):
    at = left.index(bit)
    columns = total.shape[-1]
    pre, rows = 1 << at, piece << (len(left) - at - 1)
    got = len(received)
    received = [part.reshape(2 * pre // got, rows, columns) for part in received]
    keep, *send = call(
        lambda *refs: fold_kernel(bit, got, *refs),
        "fold",
        place,
        [total.reshape(pre, 2, rows, columns), *received],
        [((pre, rows, columns), F32)] + [((pre // parts, rows, columns), BF)] * parts,
    )
    return keep, (send if parts > 1 else send[0])


def summed_up(place, keep, send, order, left, piece, gates={}):
    received = exchange(send, order[0])
    sent = []
    for step, bit in enumerate(order[1:]):
        keep, send = fold_of(
            after(place, *gates.get(step, ())), keep, [received], left, bit, piece
        )
        left = [b for b in left if b != bit]
        sent.append(send)
        received = exchange(send, bit)
    columns = keep.shape[-1]
    return keep.reshape(piece, columns), received.reshape(piece, columns), sent


def ready_kernel(gw, piece, place_ref, weight_ref, input_ref, spread_ref, keep_ref, send_ref):
    shards, _, _, step = spread_ref.shape
    positions = input_ref.shape[0]
    source = lax.broadcasted_iota(jnp.int32, (gw, step), 0)
    column = lax.broadcasted_iota(jnp.int32, (gw, step), 1) % gw
    chooser = jnp.where(source == column, 1.0, 0.0).astype(BF)
    row_group = lax.broadcasted_iota(jnp.int32, (step, step), 0) // gw
    column_group = lax.broadcasted_iota(jnp.int32, (step, step), 1) // gw
    mine = row_group == column_group
    for shard in range(shards):
        here = slice(shard * step, (shard + 1) * step)
        for tap in range(TAPS):
            copies = lax.dot_general(
                weight_ref[tap * gw : (tap + 1) * gw, here],
                chooser,
                (((0,), (0,)), ((), ())),
                preferred_element_type=F32,
            )
            spread_ref[shard, tap // 3, (tap % 3) * step : (tap % 3 + 1) * step, :] = jnp.where(
                mine, copies, 0.0
            ).astype(BF)
        turned = input_ref[:, here]
        if piece % 16:
            turned = turned.astype(F32)
        turned = turned.T.reshape(step // (2 * piece), 2, piece, positions)
        keep, send = halves(turned, place_ref[0])
        here = slice(shard * step // 2, (shard + 1) * step // 2)
        keep_ref[here, :] = keep.reshape(step // 2, positions).astype(BF)
        send_ref[here, :] = send.reshape(step // 2, positions).astype(BF)


def ready_of(place, group_weight, input_rows, shard, gw, piece):
    positions, channels = input_rows.shape
    turned = ((channels // 2, positions), BF)
    return call(
        lambda *refs: ready_kernel(gw, piece, *refs),
        "ready",
        place,
        [group_weight, input_rows],
        [((channels // shard, 3, 3 * shard, shard), BF), turned, turned],
    )


def shifted(line, left, right):
    wide = line.astype(F32)
    width = wide.shape[0]
    at = lax.broadcasted_iota(jnp.int32, wide.shape, 0)
    return (
        jnp.where(at == width - 1, right, pltpu.roll(wide, width - 1, 0)).astype(BF),
        line,
        jnp.where(at == 0, left, pltpu.roll(wide, 1, 0)).astype(BF),
    )


def own_groups(term, gw):
    step = term.shape[1]
    lane_group = lax.broadcasted_iota(jnp.int32, (gw, step), 1) // gw
    mine = term[:gw]
    for group in range(1, step // gw):
        mine = jnp.where(lane_group == group, term[group * gw : (group + 1) * gw], mine)
    return mine


def whole(refs, positions, step):
    return jnp.concatenate([ref[...].reshape(-1, step) for ref in refs])


def body_kernel(
    gw, near, place_ref, inner_ref, edge_ref, spread_ref, *refs
):
    *slots, back_ref, term_ref, window_ref = refs
    slots = slots[:1], slots[1:]
    positions, step = back_ref.shape[1:]
    width = positions // ROWS
    core = place_ref[0]
    side = place_ref[1] if near else 1 - place_ref[1]
    for slot, second_refs in enumerate(slots):
        shard = 2 * side + (core if slot == 0 else 1 - core)
        columns = pl.ds(pl.multiple_of(shard * step, step), step)
        edges = edge_ref[:, columns].astype(F32)
        for row in range(ROWS):
            here = pl.ds(row * width, width)
            edge = edges[row : row + 1]
            left, right = jnp.where(core == 1, edge, 0.0), jnp.where(core == 0, edge, 0.0)
            for at, line in enumerate(shifted(inner_ref[here, columns], left, right)):
                window_ref[here, at * step : (at + 1) * step] = line
        flipped = whole(second_refs, positions, step).T
        for tap_row in (1, 0, 2):
            count = ROWS if tap_row == 1 else ROWS - 1
            take = pl.ds(width if tap_row == 0 else 0, count * width)
            start = width if tap_row == 2 else 0
            put = pl.ds(start, count * width)
            window = window_ref[take, :]
            back = jnp.dot(window, spread_ref[shard, tap_row], preferred_element_type=F32)
            term = jnp.dot(
                flipped[:, start : start + count * width], window, preferred_element_type=F32
            )
            for tap_col in range(3):
                tap = 3 * tap_row + tap_col
                term_ref[slot, tap * gw : (tap + 1) * gw, :] = own_groups(
                    term[:, tap_col * step : (tap_col + 1) * step], gw
                )
            if tap_row == 1:
                back_ref[slot] = back
            else:
                back_ref[slot, put, :] += back


def body_of(place, near, inner, edge, own, other, spread, gw):
    positions = inner.shape[0]
    shard = own.shape[2]
    return call(
        lambda *refs: body_kernel(gw, near, *refs),
        "body_near" if near else "body_far",
        place,
        [inner, edge, spread, own, *other],
        [((2, positions, shard), F32), ((2, TAPS * gw, shard), F32)],
        [pltpu.VMEM((positions, 3 * shard), BF)],
    )


def close_kernel(
    gw, piece, near, place_ref, back_ref, term_ref, inside_ref, outside_ref,
    spread_ref, keep_in_ref, send_in_ref, *refs
):
    *slots, first_ref, keep_ref, send_ref, group_keep_ref, group_send_ref = refs
    slots = slots[:1], slots[1:]
    _, positions, step = back_ref.shape
    width = positions // ROWS
    core, half = place_ref[0], place_ref[1]
    side = half if near else 1 - half
    for slot, second_refs in enumerate(slots):
        turn = core if slot == 0 else 1 - core
        shard = 2 * side + turn
        columns = pl.ds(pl.multiple_of(shard * step, step), step)
        inside, outside = inside_ref[:, columns], outside_ref[:, columns]
        second = whole(second_refs, positions, step)
        backs, terms = {}, {}
        for tap_row, row in ((2, 0), (0, ROWS - 1)):
            rim = jnp.where(half == (0 if row == 0 else 1), outside, inside)
            edge = rim[width:].astype(F32)[0:1]
            left, right = jnp.where(core == 1, edge, 0.0), jnp.where(core == 0, edge, 0.0)
            flipped = second[row * width : (row + 1) * width].T
            window = jnp.concatenate(shifted(rim[:width], left, right), 1)
            backs[row] = jnp.dot(window, spread_ref[shard, tap_row], preferred_element_type=F32)
            term = jnp.dot(flipped, window, preferred_element_type=F32)
            terms[tap_row] = [
                own_groups(term[:, at * step : (at + 1) * step], gw) for at in range(3)
            ]
        lines = []
        for row in range(ROWS):
            here = slice(row * width, (row + 1) * width)
            back = back_ref[slot, here, :]
            if row in backs:
                back = back + backs[row]
            lines.append(jnp.where(second[here] > 0, back, 0.0).astype(BF))
        first = jnp.concatenate(lines)
        place_at = pl.ds(pl.multiple_of(turn * step, step), step)
        first_ref[:, place_at] = first
        keep_ref[:, place_at] = jnp.dot(keep_in_ref[...], first, preferred_element_type=F32)
        send_ref[:, place_at] = jnp.dot(
            send_in_ref[...], first, preferred_element_type=F32
        ).astype(BF)
        term = term_ref[slot]
        parts = []
        for tap_row in range(3):
            part = term[3 * tap_row * gw : 3 * (tap_row + 1) * gw]
            if tap_row in terms:
                part = part + jnp.concatenate(terms[tap_row])
            parts.append(part)
        turned = jnp.concatenate(parts).T.reshape(step // (2 * piece), 2, piece, TAPS * gw)
        keep, send = halves(turned, core)
        here = pl.ds(pl.multiple_of(turn * (step // 2), step // 2), step // 2)
        group_keep_ref[here, :] = keep.reshape(step // 2, TAPS * gw)
        group_send_ref[here, :] = send.reshape(step // 2, TAPS * gw).astype(BF)


def closes_kernel(
    gw, piece, count, place_ref, near_back_ref, near_term_ref, far_back_ref, far_term_ref, *refs
):
    shared, refs = refs[:5], refs[5:]
    slots, outs = refs[:-10], refs[-10:]
    for near, terms, mine, results in (
        (True, (near_back_ref, near_term_ref), slots[:count], outs[:5]),
        (False, (far_back_ref, far_term_ref), slots[count:], outs[5:]),
    ):
        close_kernel(gw, piece, near, place_ref, *terms, *shared, *mine, *results)


def closes_of(place, near, near_slots, far, far_slots, shared, piece):
    _, positions, shard = near[0].shape
    rows = shared[-1].shape[0]
    taps_gw = near[1].shape[1]
    outs = [
        ((positions, 2 * shard), BF),
        ((rows, 2 * shard), F32),
        ((rows, 2 * shard), BF),
        ((shard, taps_gw), F32),
        ((shard, taps_gw), BF),
    ]
    return call(
        lambda *refs: closes_kernel(taps_gw // TAPS, piece, len(near_slots), *refs),
        "close",
        place,
        [*near, *far, *shared, *near_slots, *far_slots],
        outs * 2,
        megabytes=14,
    )


def both_halves(half, near_ref, far_ref, near_got_ref, far_got_ref, here):
    near = near_ref[here, :] + near_got_ref[here, :].astype(F32)
    far = far_ref[here, :] + far_got_ref[here, :].astype(F32)
    return jnp.where(half == 0, near, far), jnp.where(half == 0, far, near)


def split_kernel(
    cut, piece, place_ref, near_ref, far_ref, near_got_ref, far_got_ref, keep_ref, send_ref
):
    size = 4 * piece
    for at in range(keep_ref.shape[0]):
        here = slice(at * size, (at + 1) * size)
        low, high = both_halves(
            place_ref[1], near_ref, far_ref, near_got_ref, far_got_ref, here
        )
        edge = low.shape[1] - cut
        for columns, value in ((slice(0, edge), low[:, cut:]), (slice(edge, None), high)):
            keep, send = halves(value.reshape(2, 2, piece, value.shape[1]), place_ref[1])
            rows = (size // 2, value.shape[1])
            keep_ref[at, :, columns] = keep.reshape(rows)
            send_ref[at, :, columns] = send.reshape(rows).astype(BF)


def split_group_kernel(cut, piece, place_ref, *refs):
    *wide, near_ref, far_ref, near_got_ref, far_got_ref, keep_ref, send_ref = refs
    half = place_ref[1]
    pre = keep_ref.shape[0]
    size = 4 * piece
    for at in range(pre):
        there = slice(at % (pre // 2) * size, (at % (pre // 2) + 1) * size)
        value = jnp.where(
            half == at // (pre // 2),
            near_ref[there, :] + near_got_ref[there, :].astype(F32),
            far_ref[there, :] + far_got_ref[there, :].astype(F32),
        )
        parts = [(slice(cut, None), value)]
        if cut:
            low, _ = both_halves(half, *wide, slice(at * size, (at + 1) * size))
            parts.append((slice(0, cut), low[:, :cut]))
        for columns, value in parts:
            keep, send = halves(value.reshape(1, 2, size // 2, value.shape[1]), place_ref[2])
            keep_ref[at, :, columns] = keep[0]
            send_ref[at, :, columns] = send[0].astype(BF)


def split_of(place, near, far, near_got, far_got, cut, piece):
    rows, columns = near.shape
    out = (rows // (4 * piece), 2 * piece, 2 * columns - cut)
    return call(
        lambda *refs: split_kernel(cut, piece, *refs),
        "split",
        place,
        [near, far, near_got, far_got],
        [(out, F32), (out, BF)],
    )


def split_group_of(place, wide, group, cut, piece):
    rows = wide[0].shape[0]
    out = (rows // (4 * piece), 2 * piece, cut + group[0].shape[1])
    return call(
        lambda *refs: split_group_kernel(cut, piece, *refs),
        "split_group",
        place,
        [*(wide if cut else ()), *group],
        [(out, F32), (out, BF)],
    )


def last_kernel(scale, place_ref, one_ref, one_got_ref, two_ref, two_got_ref, first_ref, group_ref):
    one = (one_ref[...] + one_got_ref[...].astype(F32)) * scale
    cut = one.shape[1] - group_ref.shape[1]
    if cut:
        first_ref[:, :cut] = one[:, :cut]
    group_ref[...] = one[:, cut:]
    first_ref[:, cut:] = (two_ref[...] + two_got_ref[...].astype(F32)) * scale


def last_of(place, scale, one, one_got, two, two_got, channels, group_columns):
    piece = one.shape[0]
    return call(
        lambda *refs: last_kernel(scale, *refs),
        "last",
        place,
        [one, one_got, two, two_got],
        [((piece, channels), F32), ((piece, group_columns), F32)],
        pinned=False,
    )


def result_kernel(place_ref, near_ref, far_ref, grad_ref, weight_ref, out_hbm, out_ref, sems):
    channels = grad_ref.shape[1]
    step = channels // 4
    halfway = channels // 2
    near = pl.ds(pl.multiple_of(place_ref[1] * halfway, halfway), halfway)
    far = pl.ds(pl.multiple_of((1 - place_ref[1]) * halfway, halfway), halfway)
    outs = []
    for part in range(4):
        here = slice(part * step, (part + 1) * step)
        summed = nt_dot(near_ref[...], weight_ref[here, near])
        summed += nt_dot(far_ref[...], weight_ref[here, far])
        out_ref[:, here] = (summed + grad_ref[:, here].astype(F32)).astype(BF)
        columns = pl.ds(part * step, step)
        outs.append(
            pltpu.make_async_copy(out_ref.at[:, columns], out_hbm.at[:, columns], sems.at[part])
        )
        outs[-1].start()
    for out in outs:
        out.wait()


def result_of(place, near, far, first_weight, grad_rows):
    rows, channels = grad_rows.shape
    vmem, hbm = (pl.BlockSpec(memory_space=kind) for kind in (pltpu.VMEM, pltpu.HBM))
    return pl.pallas_call(
        result_kernel,
        in_specs=[pl.BlockSpec(memory_space=pltpu.SMEM), vmem, vmem, vmem, vmem],
        out_specs=hbm,
        out_shape=jax.ShapeDtypeStruct((rows, channels), BF),
        scratch_shapes=[pltpu.VMEM((rows, channels), BF), pltpu.SemaphoreType.DMA((4,))],
        compiler_params=pltpu.CompilerParams(vmem_limit_bytes=12 * 1024 * 1024),
        cost_estimate=pl.CostEstimate(flops=0, bytes_accessed=0, transcendentals=0),
        name="result",
    )(place, near, far, grad_rows, first_weight)


def per_device(
    outer_grad, block_input, third_input, second_input, third_weight, group_weight, first_weight
):
    devices = lax.axis_size("space")
    position = lax.axis_index("space")
    n_bits = devices.bit_length() - 1
    place = (position >> jnp.arange(n_bits, dtype=jnp.int32)) & 1
    place = place.astype(jnp.int32)
    _, tile_rows, width, channels = outer_grad.shape
    positions = tile_rows * width
    shard = channels // 4
    gw = group_weight.shape[1] // TAPS
    piece = channels // devices
    normalizer = 1.0 / math.sqrt(positions * devices)
    grad_rows = outer_grad.reshape(positions, channels)
    third_rows = third_input.reshape(positions, channels)
    input_rows = block_input.reshape(positions, channels)
    left = list(range(n_bits - 1, 0, -1))
    z_first = [*range(2, n_bits), 1]
    x_first = [*range(1, n_bits)]

    (
        kept, sent, third_copy, grad_copy, weight_copy,
        near_own, near_core, far, edge,
    ) = front_of(place, third_rows, grad_rows, third_weight, second_input, piece)
    edge_got = exchange(edge, 0)
    near_other = exchange(near_core, 0)
    far = exchange(far, 1)
    got = exchange(sent, 0)

    kept, sent_parts = fold_of(place, kept, [got], left, 2, piece, parts=2)
    sent = sent_parts[0]
    inner, edge, inside, outside = inner_of(
        after(place, sent), grad_copy, weight_copy, third_copy, edge_got
    )
    outside = exchange_across(outside)
    inside = exchange(inside, 1)

    spread, keep_in, send_in = ready_of(
        after(place, sent), group_weight.T, input_rows, shard, gw, piece
    )
    near = body_of(place, True, inner, edge, near_own, (near_other,), spread, gw)
    far_own = far[0]
    far_other = tuple(exchange(far[1, r : r + ROWS // 2], 0) for r in (0, ROWS // 2))
    far = body_of(after(place, near[0]), False, inner, edge, far_own, far_other, spread, gw)

    order = z_first
    left_after = [b for b in left if b != 2]
    got = [exchange(part, 2) for part in sent_parts]
    kept, sent = fold_of(after(place, near[0]), kept, got, left_after, order[1], piece)
    closing = place
    left_after.remove(order[1])
    got = exchange(sent, order[1])
    kept, sent = fold_of(place, kept, [got], left_after, order[2], piece)
    splitting = after(place, sent)
    left_after.remove(order[2])

    (
        near_first, near_kept, near_send, group_near_kept, group_near_send,
        far_first, far_kept, far_send, group_far_kept, group_far_send,
    ) = closes_of(
        closing, near, (near_own, near_other), far, (far_own, *far_other),
        (inside, outside, spread, keep_in, send_in), piece,
    )
    near_got = exchange(after(near_send, sent), 0)
    group_near_got = exchange(group_near_send, 0)
    far_got = exchange(far_send, 0)
    group_far_got = exchange(group_far_send, 0)

    cut = shard // 2
    wide = (near_kept, far_kept, near_got, far_got)
    two_kept, two_sent = split_of(place, *wide, cut, piece)
    one_kept, one_sent = split_group_of(
        place, wide, (group_near_kept, group_far_kept, group_near_got, group_far_got), cut, piece
    )
    third_sent = sent
    kept, got, _ = summed_up(place, kept, sent, order[2:], left_after, piece)
    third_wgrad = (kept + got.astype(F32)) * normalizer
    input_grad = result_of(place, near_first, far_first, first_weight, grad_copy)
    *two, two_sent = summed_up(
        place, two_kept, two_sent, x_first, [b for b in left if b != 1], piece, {0: (input_grad,)}
    )
    *one, _ = summed_up(
        place, one_kept, one_sent, z_first, [b for b in left if b != 2], piece, {len(z_first) - 2: (two_sent[-1],)}
    )
    first_wgrad, group_wgrad = last_of(place, normalizer, *one, *two, channels, TAPS * gw)
    return (input_grad.reshape(outer_grad.shape), third_wgrad, group_wgrad, first_wgrad)


def solution(mesh):
    tiles = P(("parts", "space"), None, None, None)
    rows = P(("parts", "space"), None)
    return jax.shard_map(
        per_device,
        mesh=mesh,
        in_specs=(tiles, tiles, tiles, tiles, P(), P(), P()),
        out_specs=(tiles, rows, rows, rows),
        check_vma=False,
    )
```

```python
import math

import jax
import jax.numpy as jnp
from jax import lax
from jax.experimental import pallas as pl
from jax.experimental.pallas import tpu as pltpu
from jax.sharding import PartitionSpec as P

BF = jnp.bfloat16
F32 = jnp.float32
TAPS = 9
ROWS = 4


def exchange(array, bit):
    count = lax.axis_size("space")
    return lax.ppermute(array, "space", [(i, i ^ (1 << bit)) for i in range(count)])


def exchange_across(array):
    count = lax.axis_size("space")
    route = []
    for low in range(count):
        high = low + 2
        if low & 2 and high < count:
            route += [(low, high), (high, low)]
    return lax.ppermute(array, "space", route)


def after(value, *others):
    return value if not others else lax.optimization_barrier((value, *others))[0]


def call(kernel, name, place, operands, outs, scratch=(), megabytes=12, pinned=True):
    inputs, specs = [], [pl.BlockSpec(memory_space=pltpu.SMEM)]
    for operand in operands:
        if isinstance(operand, tuple):
            inputs.append(pltpu.with_memory_space_constraint(operand[0], pltpu.HBM))
            specs.append(pl.BlockSpec(memory_space=pltpu.HBM))
        else:
            inputs.append(operand)
            specs.append(pl.BlockSpec(memory_space=pltpu.VMEM))
    kind = pltpu.VMEM if pinned else jax.ShapeDtypeStruct
    return pl.pallas_call(
        kernel,
        in_specs=specs,
        out_specs=[pl.BlockSpec(memory_space=pltpu.VMEM)] * len(outs),
        out_shape=[kind(*out) for out in outs],
        scratch_shapes=scratch,
        compiler_params=pltpu.CompilerParams(vmem_limit_bytes=megabytes * 1024 * 1024),
        cost_estimate=pl.CostEstimate(flops=0, bytes_accessed=0, transcendentals=0),
        name=name,
    )(place, *inputs)


def bit_of(place_ref, bit):
    return (place_ref[0] >> bit) & 1


def nt_dot(a, b):
    return lax.dot_general(a, b, (((1,), (1,)), ((), ())), preferred_element_type=F32)


def halves(value, bit):
    low, high = value[:, 0], value[:, 1]
    return jnp.where(bit == 0, low, high), jnp.where(bit == 0, high, low)


def inner_kernel(
    place_ref, grad_ref, weight_ref, mask_ref, edge_ref,
    out_ref, rim_ref, inside_ref, outside_ref,
):
    channels = weight_ref.shape[0]
    step = channels // 2
    width = grad_ref.shape[0] // ROWS
    half = bit_of(place_ref, 1)
    for part in range(2):
        here = slice(part * step, (part + 1) * step)
        weight = weight_ref[here, :]
        back = nt_dot(grad_ref[...], weight)
        inner = jnp.where(mask_ref[:, here] > 0, back, 0.0).astype(BF)
        out_ref[:, here] = inner
        beside = nt_dot(edge_ref[...], weight)
        kept = edge_ref[:, here].astype(F32)
        lines = [
            jnp.where(kept[ROWS + row : ROWS + row + 1] > 0, beside[row : row + 1], 0.0)
            for row in range(ROWS)
        ]
        nothing = [jnp.zeros_like(lines[0])]
        rim_ref[:, here] = jnp.concatenate(lines + nothing * (16 - ROWS)).astype(BF)
        first, last = inner[:width], inner[(ROWS - 1) * width :]
        upper = jnp.concatenate([lines[0]] + nothing * 15).astype(BF)
        lower = jnp.concatenate([lines[-1]] + nothing * 15).astype(BF)
        inside_ref[:width, here] = jnp.where(half == 0, last, first)
        inside_ref[width:, here] = jnp.where(half == 0, lower, upper)
        outside_ref[:width, here] = jnp.where(half == 0, first, last)
        outside_ref[width:, here] = jnp.where(half == 0, upper, lower)


def inner_of(place, grad_rows, third_weight, third_rows, edge):
    rows, channels = grad_rows.shape
    rim = ((rows // ROWS + 16, channels), BF)
    return call(
        inner_kernel,
        "inner",
        place,
        [grad_rows, third_weight, third_rows, edge],
        [((rows, channels), BF), ((16, channels), BF), rim, rim],
    )


def front_kernel(
    piece, place_ref, left_hbm, right_hbm, weight_hbm, second_hbm,
    keep_ref, send_ref, left_ref, right_ref, weight_ref,
    near_own_ref, near_core_ref, far_ref, edge_ref, sems,
):
    rows, width, _ = near_own_ref.shape
    core, half = bit_of(place_ref, 0), bit_of(place_ref, 1)
    copies = [(left_hbm, left_ref), (right_hbm, right_ref)]
    for target, row_at, column_at in (
        (far_ref.at[0], 1 - half, core),
        (far_ref.at[1], 1 - half, 1 - core),
        (near_core_ref, half, 1 - core),
        (near_own_ref, half, core),
    ):
        source = second_hbm.at[0, pl.ds(row_at * rows, rows), pl.ds(column_at * width, width)]
        copies.append((source, target))
    copies.append((weight_hbm, weight_ref))
    copies = [pltpu.make_async_copy(*pair, sems.at[at]) for at, pair in enumerate(copies)]
    for copy in copies:
        copy.start()
    copies[0].wait()
    copies[1].wait()
    channels = left_ref.shape[1]
    step = channels // 4
    for part in range(4):
        term = lax.dot_general(
            left_ref[:, part * step : (part + 1) * step],
            right_ref[...],
            (((0,), (0,)), ((), ())),
            preferred_element_type=F32,
        )
        columns = term.shape[1]
        keep, send = halves(term.reshape(step // (2 * piece), 2, piece, columns), core)
        here = slice(part * step // 2, (part + 1) * step // 2)
        keep_ref[here, :] = keep.reshape(step // 2, columns)
        send_ref[here, :] = send.reshape(step // 2, columns).astype(BF)
    lines = []
    for value_ref in (right_ref, left_ref):
        for row in range(ROWS):
            first = value_ref[row * width : row * width + 16, :].astype(F32)[0:1]
            last = value_ref[(row + 1) * width - 16 : (row + 1) * width, :].astype(F32)[15:16]
            lines.append(jnp.where(core == 0, last, first))
    lines += [jnp.zeros_like(lines[0])] * (16 - 2 * ROWS)
    edge_ref[...] = jnp.concatenate(lines).astype(BF)
    for copy in copies[2:]:
        copy.wait()


def front_of(place, third_rows, grad_rows, third_weight, second_input, piece):
    positions, channels = grad_rows.shape
    _, rows, columns, shard = second_input.shape
    wide = ((positions, channels), BF)
    quarter = (rows // 2, columns // 2, shard)
    return call(
        lambda *refs: front_kernel(piece, *refs),
        "front",
        place,
        [(third_rows,), (grad_rows,), (third_weight,), (second_input,)],
        [
            ((channels // 2, channels), F32),
            ((channels // 2, channels), BF),
            wide,
            wide,
            ((channels, channels), BF),
            (quarter, BF),
            (quarter, BF),
            ((2, *quarter), BF),
            ((16, channels), BF),
        ],
        [pltpu.SemaphoreType.DMA((7,))],
    )


def fold_kernel(bit, got, place_ref, total_ref, *refs):
    received_refs, (keep_ref, *send_refs) = refs[:got], refs[got:]
    pre = total_ref.shape[0]
    for at in range(pre):
        pair = []
        for side in range(2):
            which, row = divmod(2 * at + side, 2 * pre // got)
            pair.append(total_ref[at, side] + received_refs[which][row].astype(F32))
        low, high = pair
        keep_ref[at] = jnp.where(bit_of(place_ref, bit) == 0, low, high)
        which, row = divmod(at, pre // len(send_refs))
        send_refs[which][row] = jnp.where(bit_of(place_ref, bit) == 0, high, low).astype(BF)


def fold_of(place, total, received, left, bit, piece, parts=1):
    at = left.index(bit)
    columns = total.shape[-1]
    pre, rows = 1 << at, piece << (len(left) - at - 1)
    got = len(received)
    received = [part.reshape(2 * pre // got, rows, columns) for part in received]
    keep, *send = call(
        lambda *refs: fold_kernel(bit, got, *refs),
        "fold",
        place,
        [total.reshape(pre, 2, rows, columns), *received],
        [((pre, rows, columns), F32)] + [((pre // parts, rows, columns), BF)] * parts,
    )
    return keep, (send if parts > 1 else send[0])


def summed_up(place, keep, send, order, left, piece, gates={}):
    received = exchange(send, order[0])
    sent = []
    for step, bit in enumerate(order[1:]):
        keep, send = fold_of(
            after(place, *gates.get(step, ())), keep, [received], left, bit, piece
        )
        left = [b for b in left if b != bit]
        sent.append(send)
        received = exchange(send, bit)
    columns = keep.shape[-1]
    return keep.reshape(piece, columns), received.reshape(piece, columns), sent


def ready_kernel(gw, piece, place_ref, weight_ref, input_ref, spread_ref, keep_ref, send_ref):
    shards, _, _, step = spread_ref.shape
    positions = input_ref.shape[0]
    source = lax.broadcasted_iota(jnp.int32, (gw, step), 0)
    column = lax.broadcasted_iota(jnp.int32, (gw, step), 1) % gw
    chooser = jnp.where(source == column, 1.0, 0.0).astype(BF)
    row_group = lax.broadcasted_iota(jnp.int32, (step, step), 0) // gw
    column_group = lax.broadcasted_iota(jnp.int32, (step, step), 1) // gw
    mine = row_group == column_group
    for shard in range(shards):
        here = slice(shard * step, (shard + 1) * step)
        for tap in range(TAPS):
            copies = lax.dot_general(
                weight_ref[tap * gw : (tap + 1) * gw, here],
                chooser,
                (((0,), (0,)), ((), ())),
                preferred_element_type=F32,
            )
            spread_ref[shard, tap // 3, (tap % 3) * step : (tap % 3 + 1) * step, :] = jnp.where(
                mine, copies, 0.0
            ).astype(BF)
        turned = input_ref[:, here]
        if piece % 16:
            turned = turned.astype(F32)
        turned = turned.T.reshape(step // (2 * piece), 2, piece, positions)
        keep, send = halves(turned, bit_of(place_ref, 0))
        here = slice(shard * step // 2, (shard + 1) * step // 2)
        keep_ref[here, :] = keep.reshape(step // 2, positions).astype(BF)
        send_ref[here, :] = send.reshape(step // 2, positions).astype(BF)


def ready_of(place, group_weight, input_rows, shard, gw, piece):
    positions, channels = input_rows.shape
    turned = ((channels // 2, positions), BF)
    return call(
        lambda *refs: ready_kernel(gw, piece, *refs),
        "ready",
        place,
        [group_weight, input_rows],
        [((channels // shard, 3, 3 * shard, shard), BF), turned, turned],
    )


def shifted(line, left, right):
    wide = line.astype(F32)
    width = wide.shape[0]
    at = lax.broadcasted_iota(jnp.int32, wide.shape, 0)
    return (
        jnp.where(at == width - 1, right, pltpu.roll(wide, width - 1, 0)).astype(BF),
        line,
        jnp.where(at == 0, left, pltpu.roll(wide, 1, 0)).astype(BF),
    )


def own_groups(term, gw):
    step = term.shape[1]
    lane_group = lax.broadcasted_iota(jnp.int32, (gw, step), 1) // gw
    mine = term[:gw]
    for group in range(1, step // gw):
        mine = jnp.where(lane_group == group, term[group * gw : (group + 1) * gw], mine)
    return mine


def whole(refs, positions, step):
    return jnp.concatenate([ref[...].reshape(-1, step) for ref in refs])


def body_kernel(
    gw, near, place_ref, inner_ref, edge_ref, spread_ref, *refs
):
    *slots, back_ref, term_ref, window_ref = refs
    slots = slots[:1], slots[1:]
    positions, step = back_ref.shape[1:]
    width = positions // ROWS
    core = bit_of(place_ref, 0)
    side = bit_of(place_ref, 1) if near else 1 - bit_of(place_ref, 1)
    for slot, second_refs in enumerate(slots):
        shard = 2 * side + (core if slot == 0 else 1 - core)
        columns = pl.ds(pl.multiple_of(shard * step, step), step)
        edges = edge_ref[:, columns].astype(F32)
        for row in range(ROWS):
            here = pl.ds(row * width, width)
            edge = edges[row : row + 1]
            left, right = jnp.where(core == 1, edge, 0.0), jnp.where(core == 0, edge, 0.0)
            for at, line in enumerate(shifted(inner_ref[here, columns], left, right)):
                window_ref[here, at * step : (at + 1) * step] = line
        flipped = whole(second_refs, positions, step).T
        for tap_row in (1, 0, 2):
            count = ROWS if tap_row == 1 else ROWS - 1
            take = pl.ds(width if tap_row == 0 else 0, count * width)
            start = width if tap_row == 2 else 0
            put = pl.ds(start, count * width)
            window = window_ref[take, :]
            back = jnp.dot(window, spread_ref[shard, tap_row], preferred_element_type=F32)
            term = jnp.dot(
                flipped[:, start : start + count * width], window, preferred_element_type=F32
            )
            for tap_col in range(3):
                tap = 3 * tap_row + tap_col
                term_ref[slot, tap * gw : (tap + 1) * gw, :] = own_groups(
                    term[:, tap_col * step : (tap_col + 1) * step], gw
                )
            if tap_row == 1:
                back_ref[slot] = back
            else:
                back_ref[slot, put, :] += back


def body_of(place, near, inner, edge, own, other, spread, gw):
    positions = inner.shape[0]
    shard = own.shape[2]
    return call(
        lambda *refs: body_kernel(gw, near, *refs),
        "body_near" if near else "body_far",
        place,
        [inner, edge, spread, own, *other],
        [((2, positions, shard), F32), ((2, TAPS * gw, shard), F32)],
        [pltpu.VMEM((positions, 3 * shard), BF)],
    )


def close_kernel(
    gw, piece, near, place_ref, back_ref, term_ref, inside_ref, outside_ref,
    spread_ref, keep_in_ref, send_in_ref, *refs
):
    *slots, first_ref, keep_ref, send_ref, group_keep_ref, group_send_ref = refs
    slots = slots[:1], slots[1:]
    _, positions, step = back_ref.shape
    width = positions // ROWS
    core, half = bit_of(place_ref, 0), bit_of(place_ref, 1)
    side = half if near else 1 - half
    for slot, second_refs in enumerate(slots):
        turn = core if slot == 0 else 1 - core
        shard = 2 * side + turn
        columns = pl.ds(pl.multiple_of(shard * step, step), step)
        inside, outside = inside_ref[:, columns], outside_ref[:, columns]
        second = whole(second_refs, positions, step)
        backs, terms = {}, {}
        for tap_row, row in ((2, 0), (0, ROWS - 1)):
            rim = jnp.where(half == (0 if row == 0 else 1), outside, inside)
            edge = rim[width:].astype(F32)[0:1]
            left, right = jnp.where(core == 1, edge, 0.0), jnp.where(core == 0, edge, 0.0)
            flipped = second[row * width : (row + 1) * width].T
            window = jnp.concatenate(shifted(rim[:width], left, right), 1)
            backs[row] = jnp.dot(window, spread_ref[shard, tap_row], preferred_element_type=F32)
            term = jnp.dot(flipped, window, preferred_element_type=F32)
            terms[tap_row] = [
                own_groups(term[:, at * step : (at + 1) * step], gw) for at in range(3)
            ]
        lines = []
        for row in range(ROWS):
            here = slice(row * width, (row + 1) * width)
            back = back_ref[slot, here, :]
            if row in backs:
                back = back + backs[row]
            lines.append(jnp.where(second[here] > 0, back, 0.0).astype(BF))
        first = jnp.concatenate(lines)
        place_at = pl.ds(pl.multiple_of(turn * step, step), step)
        first_ref[:, place_at] = first
        keep_ref[:, place_at] = jnp.dot(keep_in_ref[...], first, preferred_element_type=F32)
        send_ref[:, place_at] = jnp.dot(
            send_in_ref[...], first, preferred_element_type=F32
        ).astype(BF)
        term = term_ref[slot]
        parts = []
        for tap_row in range(3):
            part = term[3 * tap_row * gw : 3 * (tap_row + 1) * gw]
            if tap_row in terms:
                part = part + jnp.concatenate(terms[tap_row])
            parts.append(part)
        turned = jnp.concatenate(parts).T.reshape(step // (2 * piece), 2, piece, TAPS * gw)
        keep, send = halves(turned, core)
        here = pl.ds(pl.multiple_of(turn * (step // 2), step // 2), step // 2)
        group_keep_ref[here, :] = keep.reshape(step // 2, TAPS * gw)
        group_send_ref[here, :] = send.reshape(step // 2, TAPS * gw).astype(BF)


def closes_kernel(
    gw, piece, count, place_ref, near_back_ref, near_term_ref, far_back_ref, far_term_ref, *refs
):
    shared, refs = refs[:5], refs[5:]
    slots, outs = refs[:-10], refs[-10:]
    for near, terms, mine, results in (
        (True, (near_back_ref, near_term_ref), slots[:count], outs[:5]),
        (False, (far_back_ref, far_term_ref), slots[count:], outs[5:]),
    ):
        close_kernel(gw, piece, near, place_ref, *terms, *shared, *mine, *results)


def closes_of(place, near, near_slots, far, far_slots, shared, piece):
    _, positions, shard = near[0].shape
    rows = shared[-1].shape[0]
    taps_gw = near[1].shape[1]
    outs = [
        ((positions, 2 * shard), BF),
        ((rows, 2 * shard), F32),
        ((rows, 2 * shard), BF),
        ((shard, taps_gw), F32),
        ((shard, taps_gw), BF),
    ]
    return call(
        lambda *refs: closes_kernel(taps_gw // TAPS, piece, len(near_slots), *refs),
        "close",
        place,
        [*near, *far, *shared, *near_slots, *far_slots],
        outs * 2,
        megabytes=14,
    )


def both_halves(half, near_ref, far_ref, near_got_ref, far_got_ref, here):
    near = near_ref[here, :] + near_got_ref[here, :].astype(F32)
    far = far_ref[here, :] + far_got_ref[here, :].astype(F32)
    return jnp.where(half == 0, near, far), jnp.where(half == 0, far, near)


def split_kernel(
    cut, piece, place_ref, near_ref, far_ref, near_got_ref, far_got_ref, keep_ref, send_ref
):
    size = 4 * piece
    for at in range(keep_ref.shape[0]):
        here = slice(at * size, (at + 1) * size)
        low, high = both_halves(
            bit_of(place_ref, 1), near_ref, far_ref, near_got_ref, far_got_ref, here
        )
        edge = low.shape[1] - cut
        for columns, value in ((slice(0, edge), low[:, cut:]), (slice(edge, None), high)):
            keep, send = halves(value.reshape(2, 2, piece, value.shape[1]), bit_of(place_ref, 1))
            rows = (size // 2, value.shape[1])
            keep_ref[at, :, columns] = keep.reshape(rows)
            send_ref[at, :, columns] = send.reshape(rows).astype(BF)


def split_group_kernel(cut, piece, place_ref, *refs):
    *wide, near_ref, far_ref, near_got_ref, far_got_ref, keep_ref, send_ref = refs
    half = bit_of(place_ref, 1)
    pre = keep_ref.shape[0]
    size = 4 * piece
    for at in range(pre):
        there = slice(at % (pre // 2) * size, (at % (pre // 2) + 1) * size)
        value = jnp.where(
            half == at // (pre // 2),
            near_ref[there, :] + near_got_ref[there, :].astype(F32),
            far_ref[there, :] + far_got_ref[there, :].astype(F32),
        )
        parts = [(slice(cut, None), value)]
        if cut:
            low, _ = both_halves(half, *wide, slice(at * size, (at + 1) * size))
            parts.append((slice(0, cut), low[:, :cut]))
        for columns, value in parts:
            keep, send = halves(value.reshape(1, 2, size // 2, value.shape[1]), bit_of(place_ref, 2))
            keep_ref[at, :, columns] = keep[0]
            send_ref[at, :, columns] = send[0].astype(BF)


def split_of(place, near, far, near_got, far_got, cut, piece):
    rows, columns = near.shape
    out = (rows // (4 * piece), 2 * piece, 2 * columns - cut)
    return call(
        lambda *refs: split_kernel(cut, piece, *refs),
        "split",
        place,
        [near, far, near_got, far_got],
        [(out, F32), (out, BF)],
    )


def split_group_of(place, wide, group, cut, piece):
    rows = wide[0].shape[0]
    out = (rows // (4 * piece), 2 * piece, cut + group[0].shape[1])
    return call(
        lambda *refs: split_group_kernel(cut, piece, *refs),
        "split_group",
        place,
        [*(wide if cut else ()), *group],
        [(out, F32), (out, BF)],
    )


def last_kernel(scale, place_ref, one_ref, one_got_ref, two_ref, two_got_ref, first_ref, group_ref):
    one = (one_ref[...] + one_got_ref[...].astype(F32)) * scale
    cut = one.shape[1] - group_ref.shape[1]
    if cut:
        first_ref[:, :cut] = one[:, :cut]
    group_ref[...] = one[:, cut:]
    first_ref[:, cut:] = (two_ref[...] + two_got_ref[...].astype(F32)) * scale


def last_of(place, scale, one, one_got, two, two_got, channels, group_columns):
    piece = one.shape[0]
    return call(
        lambda *refs: last_kernel(scale, *refs),
        "last",
        place,
        [one, one_got, two, two_got],
        [((piece, channels), F32), ((piece, group_columns), F32)],
        pinned=False,
    )


def result_kernel(place_ref, near_ref, far_ref, grad_ref, weight_ref, out_hbm, out_ref, sems):
    channels = grad_ref.shape[1]
    step = channels // 4
    halfway = channels // 2
    near = pl.ds(pl.multiple_of(bit_of(place_ref, 1) * halfway, halfway), halfway)
    far = pl.ds(pl.multiple_of((1 - bit_of(place_ref, 1)) * halfway, halfway), halfway)
    outs = []
    for part in range(4):
        here = slice(part * step, (part + 1) * step)
        summed = nt_dot(near_ref[...], weight_ref[here, near])
        summed += nt_dot(far_ref[...], weight_ref[here, far])
        out_ref[:, here] = (summed + grad_ref[:, here].astype(F32)).astype(BF)
        columns = pl.ds(part * step, step)
        outs.append(
            pltpu.make_async_copy(out_ref.at[:, columns], out_hbm.at[:, columns], sems.at[part])
        )
        outs[-1].start()
    for out in outs:
        out.wait()


def result_of(place, near, far, first_weight, grad_rows):
    rows, channels = grad_rows.shape
    vmem, hbm = (pl.BlockSpec(memory_space=kind) for kind in (pltpu.VMEM, pltpu.HBM))
    return pl.pallas_call(
        result_kernel,
        in_specs=[pl.BlockSpec(memory_space=pltpu.SMEM), vmem, vmem, vmem, vmem],
        out_specs=hbm,
        out_shape=jax.ShapeDtypeStruct((rows, channels), BF),
        scratch_shapes=[pltpu.VMEM((rows, channels), BF), pltpu.SemaphoreType.DMA((4,))],
        compiler_params=pltpu.CompilerParams(vmem_limit_bytes=12 * 1024 * 1024),
        cost_estimate=pl.CostEstimate(flops=0, bytes_accessed=0, transcendentals=0),
        name="result",
    )(place, near, far, grad_rows, first_weight)


def per_device(
    outer_grad, block_input, third_input, second_input, third_weight, group_weight, first_weight
):
    devices = lax.axis_size("space")
    position = lax.axis_index("space")
    n_bits = devices.bit_length() - 1
    place = position.astype(jnp.int32).reshape(1)
    _, tile_rows, width, channels = outer_grad.shape
    positions = tile_rows * width
    shard = channels // 4
    gw = group_weight.shape[1] // TAPS
    piece = channels // devices
    normalizer = 1.0 / math.sqrt(positions * devices)
    grad_rows = outer_grad.reshape(positions, channels)
    third_rows = third_input.reshape(positions, channels)
    input_rows = block_input.reshape(positions, channels)
    left = list(range(n_bits - 1, 0, -1))
    z_first = [*range(2, n_bits), 1]
    x_first = [*range(1, n_bits)]

    (
        kept, sent, third_copy, grad_copy, weight_copy,
        near_own, near_core, far, edge,
    ) = front_of(place, third_rows, grad_rows, third_weight, second_input, piece)
    edge_got = exchange(edge, 0)
    near_other = exchange(near_core, 0)
    far = exchange(far, 1)
    got = exchange(sent, 0)

    kept, sent_parts = fold_of(place, kept, [got], left, 2, piece, parts=2)
    sent = sent_parts[0]
    inner, edge, inside, outside = inner_of(
        after(place, sent), grad_copy, weight_copy, third_copy, edge_got
    )
    outside = exchange_across(outside)
    inside = exchange(inside, 1)

    spread, keep_in, send_in = ready_of(
        after(place, sent), group_weight.T, input_rows, shard, gw, piece
    )
    near = body_of(place, True, inner, edge, near_own, (near_other,), spread, gw)
    far_own = far[0]
    far_other = tuple(exchange(far[1, r : r + ROWS // 2], 0) for r in (0, ROWS // 2))
    far = body_of(after(place, near[0]), False, inner, edge, far_own, far_other, spread, gw)

    order = z_first
    left_after = [b for b in left if b != 2]
    got = [exchange(part, 2) for part in sent_parts]
    kept, sent = fold_of(after(place, near[0]), kept, got, left_after, order[1], piece)
    closing = place
    left_after.remove(order[1])
    got = exchange(sent, order[1])
    kept, sent = fold_of(place, kept, [got], left_after, order[2], piece)
    splitting = after(place, sent)
    left_after.remove(order[2])

    (
        near_first, near_kept, near_send, group_near_kept, group_near_send,
        far_first, far_kept, far_send, group_far_kept, group_far_send,
    ) = closes_of(
        closing, near, (near_own, near_other), far, (far_own, *far_other),
        (inside, outside, spread, keep_in, send_in), piece,
    )
    near_got = exchange(after(near_send, sent), 0)
    group_near_got = exchange(group_near_send, 0)
    far_got = exchange(far_send, 0)
    group_far_got = exchange(group_far_send, 0)

    cut = shard // 2
    wide = (near_kept, far_kept, near_got, far_got)
    two_kept, two_sent = split_of(place, *wide, cut, piece)
    one_kept, one_sent = split_group_of(
        place, wide, (group_near_kept, group_far_kept, group_near_got, group_far_got), cut, piece
    )
    third_sent = sent
    kept, got, _ = summed_up(place, kept, sent, order[2:], left_after, piece)
    third_wgrad = (kept + got.astype(F32)) * normalizer
    input_grad = result_of(place, near_first, far_first, first_weight, grad_copy)
    *two, two_sent = summed_up(
        place, two_kept, two_sent, x_first, [b for b in left if b != 1], piece, {0: (input_grad,)}
    )
    *one, _ = summed_up(
        place, one_kept, one_sent, z_first, [b for b in left if b != 2], piece, {len(z_first) - 2: (two_sent[-1],)}
    )
    first_wgrad, group_wgrad = last_of(place, normalizer, *one, *two, channels, TAPS * gw)
    return (input_grad.reshape(outer_grad.shape), third_wgrad, group_wgrad, first_wgrad)


def solution(mesh):
    tiles = P(("parts", "space"), None, None, None)
    rows = P(("parts", "space"), None)
    return jax.shard_map(
        per_device,
        mesh=mesh,
        in_specs=(tiles, tiles, tiles, tiles, P(), P(), P()),
        out_specs=(tiles, rows, rows, rows),
        check_vma=False,
    )
```

```python
import math

import jax
import jax.numpy as jnp
from jax import lax
from jax.experimental import pallas as pl
from jax.experimental.pallas import tpu as pltpu
from jax.sharding import PartitionSpec as P

BF = jnp.bfloat16
F32 = jnp.float32
TAPS = 9
ROWS = 4


def exchange(array, bit):
    count = lax.axis_size("space")
    return lax.ppermute(array, "space", [(i, i ^ (1 << bit)) for i in range(count)])


def exchange_across(array):
    count = lax.axis_size("space")
    route = []
    for low in range(count):
        high = low + 2
        if low & 2 and high < count:
            route += [(low, high), (high, low)]
    return lax.ppermute(array, "space", route)


def after(value, *others):
    return value if not others else lax.optimization_barrier((value, *others))[0]


def call(kernel, name, place, operands, outs, scratch=(), megabytes=12, pinned=True):
    inputs, specs = [], [pl.BlockSpec(memory_space=pltpu.SMEM)]
    for operand in operands:
        if isinstance(operand, tuple):
            inputs.append(pltpu.with_memory_space_constraint(operand[0], pltpu.HBM))
            specs.append(pl.BlockSpec(memory_space=pltpu.HBM))
        else:
            inputs.append(operand)
            specs.append(pl.BlockSpec(memory_space=pltpu.VMEM))
    kind = pltpu.VMEM if pinned else jax.ShapeDtypeStruct
    return pl.pallas_call(
        kernel,
        in_specs=specs,
        out_specs=[pl.BlockSpec(memory_space=pltpu.VMEM)] * len(outs),
        out_shape=[kind(*out) for out in outs],
        scratch_shapes=scratch,
        compiler_params=pltpu.CompilerParams(vmem_limit_bytes=megabytes * 1024 * 1024),
        cost_estimate=pl.CostEstimate(flops=0, bytes_accessed=0, transcendentals=0),
        name=name,
    )(place, *inputs)


def bit_of(place_ref, bit):
    return (place_ref[0] >> bit) & 1


def nt_dot(a, b):
    return lax.dot_general(a, b, (((1,), (1,)), ((), ())), preferred_element_type=F32)


def halves(value, bit):
    low, high = value[:, 0], value[:, 1]
    return jnp.where(bit == 0, low, high), jnp.where(bit == 0, high, low)


def inner_kernel(
    place_ref, grad_ref, weight_ref, mask_ref, edge_ref,
    out_ref, rim_ref, inside_ref, outside_ref,
):
    channels = weight_ref.shape[0]
    step = channels // 2
    width = grad_ref.shape[0] // ROWS
    half = bit_of(place_ref, 1)
    for part in range(2):
        here = slice(part * step, (part + 1) * step)
        weight = weight_ref[here, :]
        back = nt_dot(grad_ref[...], weight)
        inner = jnp.where(mask_ref[:, here] > 0, back, 0.0).astype(BF)
        out_ref[:, here] = inner
        beside = nt_dot(edge_ref[...], weight)
        kept = edge_ref[:, here].astype(F32)
        lines = [
            jnp.where(kept[ROWS + row : ROWS + row + 1] > 0, beside[row : row + 1], 0.0)
            for row in range(ROWS)
        ]
        nothing = [jnp.zeros_like(lines[0])]
        rim_ref[:, here] = jnp.concatenate(lines + nothing * (16 - ROWS)).astype(BF)
        first, last = inner[:width], inner[(ROWS - 1) * width :]
        upper = jnp.concatenate([lines[0]] + nothing * 15).astype(BF)
        lower = jnp.concatenate([lines[-1]] + nothing * 15).astype(BF)
        inside_ref[:width, here] = jnp.where(half == 0, last, first)
        inside_ref[width:, here] = jnp.where(half == 0, lower, upper)
        outside_ref[:width, here] = jnp.where(half == 0, first, last)
        outside_ref[width:, here] = jnp.where(half == 0, upper, lower)


def inner_of(place, grad_rows, third_weight, third_rows, edge):
    rows, channels = grad_rows.shape
    rim = ((rows // ROWS + 16, channels), BF)
    return call(
        inner_kernel,
        "inner",
        place,
        [grad_rows, third_weight, third_rows, edge],
        [((rows, channels), BF), ((16, channels), BF), rim, rim],
    )


def front_kernel(
    piece, place_ref, left_hbm, right_hbm, weight_hbm, second_hbm,
    keep_ref, send_ref, left_ref, right_ref, weight_ref,
    near_own_ref, near_core_ref, far_ref, edge_ref, sems,
):
    rows, width, _ = near_own_ref.shape
    core, half = bit_of(place_ref, 0), bit_of(place_ref, 1)
    copies = [(left_hbm, left_ref), (right_hbm, right_ref)]
    for target, row_at, column_at in (
        (far_ref.at[0], 1 - half, core),
        (far_ref.at[1], 1 - half, 1 - core),
        (near_core_ref, half, 1 - core),
        (near_own_ref, half, core),
    ):
        source = second_hbm.at[0, pl.ds(row_at * rows, rows), pl.ds(column_at * width, width)]
        copies.append((source, target))
    copies.append((weight_hbm, weight_ref))
    copies = [pltpu.make_async_copy(*pair, sems.at[at]) for at, pair in enumerate(copies)]
    for copy in copies:
        copy.start()
    copies[0].wait()
    copies[1].wait()
    channels = left_ref.shape[1]
    step = channels // 4
    for part in range(4):
        term = lax.dot_general(
            left_ref[:, part * step : (part + 1) * step],
            right_ref[...],
            (((0,), (0,)), ((), ())),
            preferred_element_type=F32,
        )
        columns = term.shape[1]
        keep, send = halves(term.reshape(step // (2 * piece), 2, piece, columns), core)
        here = slice(part * step // 2, (part + 1) * step // 2)
        keep_ref[here, :] = keep.reshape(step // 2, columns)
        send_ref[here, :] = send.reshape(step // 2, columns).astype(BF)
    lines = []
    for value_ref in (right_ref, left_ref):
        for row in range(ROWS):
            first = value_ref[row * width : row * width + 16, :].astype(F32)[0:1]
            last = value_ref[(row + 1) * width - 16 : (row + 1) * width, :].astype(F32)[15:16]
            lines.append(jnp.where(core == 0, last, first))
    lines += [jnp.zeros_like(lines[0])] * (16 - 2 * ROWS)
    edge_ref[...] = jnp.concatenate(lines).astype(BF)
    for copy in copies[2:]:
        copy.wait()


def front_of(place, third_rows, grad_rows, third_weight, second_input, piece):
    positions, channels = grad_rows.shape
    _, rows, columns, shard = second_input.shape
    wide = ((positions, channels), BF)
    quarter = (rows // 2, columns // 2, shard)
    return call(
        lambda *refs: front_kernel(piece, *refs),
        "front",
        place,
        [(third_rows,), (grad_rows,), (third_weight,), (second_input,)],
        [
            ((channels // 2, channels), F32),
            ((channels // 2, channels), BF),
            wide,
            wide,
            ((channels, channels), BF),
            (quarter, BF),
            (quarter, BF),
            ((2, *quarter), BF),
            ((16, channels), BF),
        ],
        [pltpu.SemaphoreType.DMA((7,))],
    )


def fold_kernel(bit, got, place_ref, total_ref, *refs):
    received_refs, (keep_ref, *send_refs) = refs[:got], refs[got:]
    pre = total_ref.shape[0]
    for at in range(pre):
        pair = []
        for side in range(2):
            which, row = divmod(2 * at + side, 2 * pre // got)
            pair.append(total_ref[at, side] + received_refs[which][row].astype(F32))
        low, high = pair
        keep_ref[at] = jnp.where(bit_of(place_ref, bit) == 0, low, high)
        which, row = divmod(at, pre // len(send_refs))
        send_refs[which][row] = jnp.where(bit_of(place_ref, bit) == 0, high, low).astype(BF)


def fold_of(place, total, received, left, bit, piece, parts=1):
    at = left.index(bit)
    columns = total.shape[-1]
    pre, rows = 1 << at, piece << (len(left) - at - 1)
    got = len(received)
    received = [part.reshape(2 * pre // got, rows, columns) for part in received]
    keep, *send = call(
        lambda *refs: fold_kernel(bit, got, *refs),
        "fold",
        place,
        [total.reshape(pre, 2, rows, columns), *received],
        [((pre, rows, columns), F32)] + [((pre // parts, rows, columns), BF)] * parts,
    )
    return keep, (send if parts > 1 else send[0])


def summed_up(place, keep, send, order, left, piece, gates={}):
    received = exchange(send, order[0])
    sent = []
    for step, bit in enumerate(order[1:]):
        keep, send = fold_of(
            after(place, *gates.get(step, ())), keep, [received], left, bit, piece
        )
        left = [b for b in left if b != bit]
        sent.append(send)
        received = exchange(send, bit)
    columns = keep.shape[-1]
    return keep.reshape(piece, columns), received.reshape(piece, columns), sent


def ready_kernel(gw, piece, place_ref, weight_ref, input_ref, spread_ref, keep_ref, send_ref):
    shards, _, _, step = spread_ref.shape
    positions = input_ref.shape[0]
    source = lax.broadcasted_iota(jnp.int32, (gw, step), 0)
    column = lax.broadcasted_iota(jnp.int32, (gw, step), 1) % gw
    chooser = jnp.where(source == column, 1.0, 0.0).astype(BF)
    row_group = lax.broadcasted_iota(jnp.int32, (step, step), 0) // gw
    column_group = lax.broadcasted_iota(jnp.int32, (step, step), 1) // gw
    mine = row_group == column_group
    for shard in range(shards):
        here = slice(shard * step, (shard + 1) * step)
        for tap in range(TAPS):
            copies = lax.dot_general(
                weight_ref[tap * gw : (tap + 1) * gw, here],
                chooser,
                (((0,), (0,)), ((), ())),
                preferred_element_type=F32,
            )
            spread_ref[shard, tap // 3, (tap % 3) * step : (tap % 3 + 1) * step, :] = jnp.where(
                mine, copies, 0.0
            ).astype(BF)
        turned = input_ref[:, here]
        if piece % 16:
            turned = turned.astype(F32)
        turned = turned.T.reshape(step // (2 * piece), 2, piece, positions)
        keep, send = halves(turned, bit_of(place_ref, 0))
        here = slice(shard * step // 2, (shard + 1) * step // 2)
        keep_ref[here, :] = keep.reshape(step // 2, positions).astype(BF)
        send_ref[here, :] = send.reshape(step // 2, positions).astype(BF)


def ready_of(place, group_weight, input_rows, shard, gw, piece):
    positions, channels = input_rows.shape
    turned = ((channels // 2, positions), BF)
    return call(
        lambda *refs: ready_kernel(gw, piece, *refs),
        "ready",
        place,
        [group_weight, input_rows],
        [((channels // shard, 3, 3 * shard, shard), BF), turned, turned],
    )


def shifted(line, left, right):
    wide = line.astype(F32)
    width = wide.shape[0]
    at = lax.broadcasted_iota(jnp.int32, wide.shape, 0)
    return (
        jnp.where(at == width - 1, right, pltpu.roll(wide, width - 1, 0)).astype(BF),
        line,
        jnp.where(at == 0, left, pltpu.roll(wide, 1, 0)).astype(BF),
    )


def own_groups(term, gw):
    step = term.shape[1]
    lane_group = lax.broadcasted_iota(jnp.int32, (gw, step), 1) // gw
    mine = term[:gw]
    for group in range(1, step // gw):
        mine = jnp.where(lane_group == group, term[group * gw : (group + 1) * gw], mine)
    return mine


def whole(refs, positions, step):
    return jnp.concatenate([ref[...].reshape(-1, step) for ref in refs])


def body_kernel(
    gw, near, place_ref, inner_ref, edge_ref, spread_ref, *refs
):
    *slots, back_ref, term_ref, window_ref = refs
    slots = slots[:1], slots[1:]
    positions, step = back_ref.shape[1:]
    width = positions // ROWS
    core = bit_of(place_ref, 0)
    side = bit_of(place_ref, 1) if near else 1 - bit_of(place_ref, 1)
    for slot, second_refs in enumerate(slots):
        shard = 2 * side + (core if slot == 0 else 1 - core)
        columns = pl.ds(pl.multiple_of(shard * step, step), step)
        edges = edge_ref[:, columns].astype(F32)
        for row in range(ROWS):
            here = pl.ds(row * width, width)
            edge = edges[row : row + 1]
            left, right = jnp.where(core == 1, edge, 0.0), jnp.where(core == 0, edge, 0.0)
            for at, line in enumerate(shifted(inner_ref[here, columns], left, right)):
                window_ref[here, at * step : (at + 1) * step] = line
        flipped = whole(second_refs, positions, step).T
        for tap_row in (1, 0, 2):
            count = ROWS if tap_row == 1 else ROWS - 1
            take = pl.ds(width if tap_row == 0 else 0, count * width)
            start = width if tap_row == 2 else 0
            put = pl.ds(start, count * width)
            window = window_ref[take, :]
            back = jnp.dot(window, spread_ref[shard, tap_row], preferred_element_type=F32)
            term = jnp.dot(
                flipped[:, start : start + count * width], window, preferred_element_type=F32
            )
            for tap_col in range(3):
                tap = 3 * tap_row + tap_col
                term_ref[slot, tap * gw : (tap + 1) * gw, :] = own_groups(
                    term[:, tap_col * step : (tap_col + 1) * step], gw
                )
            if tap_row == 1:
                back_ref[slot] = back
            else:
                back_ref[slot, put, :] += back


def body_of(place, near, inner, edge, own, other, spread, gw):
    positions = inner.shape[0]
    shard = own.shape[2]
    return call(
        lambda *refs: body_kernel(gw, near, *refs),
        "body_near" if near else "body_far",
        place,
        [inner, edge, spread, own, *other],
        [((2, positions, shard), F32), ((2, TAPS * gw, shard), F32)],
        [pltpu.VMEM((positions, 3 * shard), BF)],
    )


def close_kernel(
    gw, piece, near, place_ref, back_ref, term_ref, inside_ref, outside_ref,
    spread_ref, keep_in_ref, send_in_ref, *refs
):
    *slots, first_ref, keep_ref, send_ref, group_keep_ref, group_send_ref = refs
    slots = slots[:1], slots[1:]
    _, positions, step = back_ref.shape
    width = positions // ROWS
    core, half = bit_of(place_ref, 0), bit_of(place_ref, 1)
    side = half if near else 1 - half
    for slot, second_refs in enumerate(slots):
        turn = core if slot == 0 else 1 - core
        shard = 2 * side + turn
        columns = pl.ds(pl.multiple_of(shard * step, step), step)
        inside, outside = inside_ref[:, columns], outside_ref[:, columns]
        second = whole(second_refs, positions, step)
        backs, terms = {}, {}
        for tap_row, row in ((2, 0), (0, ROWS - 1)):
            rim = jnp.where(half == (0 if row == 0 else 1), outside, inside)
            edge = rim[width:].astype(F32)[0:1]
            left, right = jnp.where(core == 1, edge, 0.0), jnp.where(core == 0, edge, 0.0)
            flipped = second[row * width : (row + 1) * width].T
            window = jnp.concatenate(shifted(rim[:width], left, right), 1)
            backs[row] = jnp.dot(window, spread_ref[shard, tap_row], preferred_element_type=F32)
            term = jnp.dot(flipped, window, preferred_element_type=F32)
            terms[tap_row] = [
                own_groups(term[:, at * step : (at + 1) * step], gw) for at in range(3)
            ]
        lines = []
        for row in range(ROWS):
            here = slice(row * width, (row + 1) * width)
            back = back_ref[slot, here, :]
            if row in backs:
                back = back + backs[row]
            lines.append(jnp.where(second[here] > 0, back, 0.0).astype(BF))
        first = jnp.concatenate(lines)
        place_at = pl.ds(pl.multiple_of(turn * step, step), step)
        first_ref[:, place_at] = first
        keep_ref[:, place_at] = jnp.dot(keep_in_ref[...], first, preferred_element_type=F32)
        send_ref[:, place_at] = jnp.dot(
            send_in_ref[...], first, preferred_element_type=F32
        ).astype(BF)
        term = term_ref[slot]
        parts = []
        for tap_row in range(3):
            part = term[3 * tap_row * gw : 3 * (tap_row + 1) * gw]
            if tap_row in terms:
                part = part + jnp.concatenate(terms[tap_row])
            parts.append(part)
        turned = jnp.concatenate(parts).T.reshape(step // (2 * piece), 2, piece, TAPS * gw)
        keep, send = halves(turned, core)
        here = pl.ds(pl.multiple_of(turn * (step // 2), step // 2), step // 2)
        group_keep_ref[here, :] = keep.reshape(step // 2, TAPS * gw)
        group_send_ref[here, :] = send.reshape(step // 2, TAPS * gw).astype(BF)


def closes_kernel(
    gw, piece, count, place_ref, near_back_ref, near_term_ref, far_back_ref, far_term_ref, *refs
):
    shared, refs = refs[:5], refs[5:]
    slots, outs = refs[:-10], refs[-10:]
    for near, terms, mine, results in (
        (True, (near_back_ref, near_term_ref), slots[:count], outs[:5]),
        (False, (far_back_ref, far_term_ref), slots[count:], outs[5:]),
    ):
        close_kernel(gw, piece, near, place_ref, *terms, *shared, *mine, *results)


def closes_of(place, near, near_slots, far, far_slots, shared, piece):
    _, positions, shard = near[0].shape
    rows = shared[-1].shape[0]
    taps_gw = near[1].shape[1]
    outs = [
        ((positions, 2 * shard), BF),
        ((rows, 2 * shard), F32),
        ((rows, 2 * shard), BF),
        ((shard, taps_gw), F32),
        ((shard, taps_gw), BF),
    ]
    return call(
        lambda *refs: closes_kernel(taps_gw // TAPS, piece, len(near_slots), *refs),
        "close",
        place,
        [*near, *far, *shared, *near_slots, *far_slots],
        outs * 2,
        megabytes=14,
    )


def both_halves(half, near_ref, far_ref, near_got_ref, far_got_ref, here):
    near = near_ref[here, :] + near_got_ref[here, :].astype(F32)
    far = far_ref[here, :] + far_got_ref[here, :].astype(F32)
    return jnp.where(half == 0, near, far), jnp.where(half == 0, far, near)


def split_kernel(
    cut, piece, place_ref, near_ref, far_ref, near_got_ref, far_got_ref, keep_ref, send_ref
):
    size = 4 * piece
    for at in range(keep_ref.shape[0]):
        here = slice(at * size, (at + 1) * size)
        low, high = both_halves(
            bit_of(place_ref, 1), near_ref, far_ref, near_got_ref, far_got_ref, here
        )
        edge = low.shape[1] - cut
        for columns, value in ((slice(0, edge), low[:, cut:]), (slice(edge, None), high)):
            keep, send = halves(value.reshape(2, 2, piece, value.shape[1]), bit_of(place_ref, 1))
            rows = (size // 2, value.shape[1])
            keep_ref[at, :, columns] = keep.reshape(rows)
            send_ref[at, :, columns] = send.reshape(rows).astype(BF)


def split_group_kernel(cut, piece, place_ref, *refs):
    *wide, near_ref, far_ref, near_got_ref, far_got_ref, keep_ref, send_ref = refs
    half = bit_of(place_ref, 1)
    pre = keep_ref.shape[0]
    size = 4 * piece
    for at in range(pre):
        there = slice(at % (pre // 2) * size, (at % (pre // 2) + 1) * size)
        value = jnp.where(
            half == at // (pre // 2),
            near_ref[there, :] + near_got_ref[there, :].astype(F32),
            far_ref[there, :] + far_got_ref[there, :].astype(F32),
        )
        parts = [(slice(cut, None), value)]
        if cut:
            low, _ = both_halves(half, *wide, slice(at * size, (at + 1) * size))
            parts.append((slice(0, cut), low[:, :cut]))
        for columns, value in parts:
            keep, send = halves(value.reshape(1, 2, size // 2, value.shape[1]), bit_of(place_ref, 2))
            keep_ref[at, :, columns] = keep[0]
            send_ref[at, :, columns] = send[0].astype(BF)


def split_of(place, near, far, near_got, far_got, cut, piece):
    rows, columns = near.shape
    out = (rows // (4 * piece), 2 * piece, 2 * columns - cut)
    return call(
        lambda *refs: split_kernel(cut, piece, *refs),
        "split",
        place,
        [near, far, near_got, far_got],
        [(out, F32), (out, BF)],
    )


def split_group_of(place, wide, group, cut, piece):
    rows = wide[0].shape[0]
    out = (rows // (4 * piece), 2 * piece, cut + group[0].shape[1])
    return call(
        lambda *refs: split_group_kernel(cut, piece, *refs),
        "split_group",
        place,
        [*(wide if cut else ()), *group],
        [(out, F32), (out, BF)],
    )


def last_kernel(scale, place_ref, one_ref, one_got_ref, two_ref, two_got_ref, first_ref, group_ref):
    one = (one_ref[...] + one_got_ref[...].astype(F32)) * scale
    cut = one.shape[1] - group_ref.shape[1]
    if cut:
        first_ref[:, :cut] = one[:, :cut]
    group_ref[...] = one[:, cut:]
    first_ref[:, cut:] = (two_ref[...] + two_got_ref[...].astype(F32)) * scale


def last_of(place, scale, one, one_got, two, two_got, channels, group_columns):
    piece = one.shape[0]
    return call(
        lambda *refs: last_kernel(scale, *refs),
        "last",
        place,
        [one, one_got, two, two_got],
        [((piece, channels), F32), ((piece, group_columns), F32)],
        pinned=False,
    )


def result_kernel(place_ref, near_ref, far_ref, grad_ref, weight_ref, out_hbm, out_ref, sems):
    channels = grad_ref.shape[1]
    step = channels // 4
    halfway = channels // 2
    near = pl.ds(pl.multiple_of(bit_of(place_ref, 1) * halfway, halfway), halfway)
    far = pl.ds(pl.multiple_of((1 - bit_of(place_ref, 1)) * halfway, halfway), halfway)
    outs = []
    for part in range(4):
        here = slice(part * step, (part + 1) * step)
        summed = nt_dot(near_ref[...], weight_ref[here, near])
        summed += nt_dot(far_ref[...], weight_ref[here, far])
        out_ref[:, here] = (summed + grad_ref[:, here].astype(F32)).astype(BF)
        columns = pl.ds(part * step, step)
        outs.append(
            pltpu.make_async_copy(out_ref.at[:, columns], out_hbm.at[:, columns], sems.at[part])
        )
        outs[-1].start()
    for out in outs:
        out.wait()


def result_of(place, near, far, first_weight, grad_rows):
    rows, channels = grad_rows.shape
    vmem, hbm = (pl.BlockSpec(memory_space=kind) for kind in (pltpu.VMEM, pltpu.HBM))
    return pl.pallas_call(
        result_kernel,
        in_specs=[pl.BlockSpec(memory_space=pltpu.SMEM), vmem, vmem, vmem, vmem],
        out_specs=hbm,
        out_shape=jax.ShapeDtypeStruct((rows, channels), BF),
        scratch_shapes=[pltpu.VMEM((rows, channels), BF), pltpu.SemaphoreType.DMA((4,))],
        compiler_params=pltpu.CompilerParams(vmem_limit_bytes=12 * 1024 * 1024),
        cost_estimate=pl.CostEstimate(flops=0, bytes_accessed=0, transcendentals=0),
        name="result",
    )(place, near, far, grad_rows, first_weight)


def per_device(
    outer_grad, block_input, third_input, second_input, third_weight, group_weight, first_weight
):
    devices = lax.axis_size("space")
    position = lax.axis_index("space")
    n_bits = devices.bit_length() - 1
    place = position.astype(jnp.int32).reshape(1)
    _, tile_rows, width, channels = outer_grad.shape
    positions = tile_rows * width
    shard = channels // 4
    gw = group_weight.shape[1] // TAPS
    piece = channels // devices
    normalizer = 1.0 / math.sqrt(positions * devices)
    grad_rows = outer_grad.reshape(positions, channels)
    third_rows = third_input.reshape(positions, channels)
    input_rows = block_input.reshape(positions, channels)
    left = list(range(n_bits - 1, 0, -1))
    z_first = [*range(2, n_bits), 1]
    x_first = [*range(1, n_bits)]

    (
        kept, sent, third_copy, grad_copy, weight_copy,
        near_own, near_core, far, edge,
    ) = front_of(place, third_rows, grad_rows, third_weight, second_input, piece)
    edge_got = exchange(edge, 0)
    near_other = exchange(near_core, 0)
    far = exchange(far, 1)
    got = exchange(sent, 0)

    kept, sent_parts = fold_of(place, kept, [got], left, 2, piece, parts=2)
    sent = sent_parts[0]
    inner, edge, inside, outside = inner_of(
        after(place, sent), grad_copy, weight_copy, third_copy, edge_got
    )
    outside = exchange_across(outside)
    inside = exchange(inside, 1)

    spread, keep_in, send_in = ready_of(
        after(place, sent), group_weight.T, input_rows, shard, gw, piece
    )
    near = body_of(place, True, inner, edge, near_own, (near_other,), spread, gw)
    far_own = far[0]
    far_other = tuple(exchange(far[1, r : r + ROWS // 2], 0) for r in (0, ROWS // 2))
    far = body_of(after(place, near[0]), False, inner, edge, far_own, far_other, spread, gw)

    order = z_first
    left_after = [b for b in left if b != 2]
    got = [exchange(part, 2) for part in sent_parts]
    kept, sent = fold_of(after(place, near[0]), kept, got, left_after, order[1], piece)
    closing = place
    left_after.remove(order[1])
    got = exchange(sent, order[1])
    kept, sent = fold_of(place, kept, [got], left_after, order[2], piece)
    splitting = after(place, sent)
    left_after.remove(order[2])

    (
        near_first, near_kept, near_send, group_near_kept, group_near_send,
        far_first, far_kept, far_send, group_far_kept, group_far_send,
    ) = closes_of(
        closing, near, (near_own, near_other), far, (far_own, *far_other),
        (inside, outside, spread, keep_in, send_in), piece,
    )
    near_got = exchange(near_send, 0)
    group_near_got = exchange(group_near_send, 0)
    far_got = exchange(after(far_send, sent), 0)
    group_far_got = exchange(group_far_send, 0)

    cut = shard // 2
    wide = (near_kept, far_kept, near_got, far_got)
    two_kept, two_sent = split_of(place, *wide, cut, piece)
    one_kept, one_sent = split_group_of(
        place, wide, (group_near_kept, group_far_kept, group_near_got, group_far_got), cut, piece
    )
    third_sent = sent
    kept, got, _ = summed_up(place, kept, sent, order[2:], left_after, piece)
    third_wgrad = (kept + got.astype(F32)) * normalizer
    input_grad = result_of(place, near_first, far_first, first_weight, grad_copy)
    *two, two_sent = summed_up(
        place, two_kept, two_sent, x_first, [b for b in left if b != 1], piece, {0: (input_grad,)}
    )
    *one, _ = summed_up(
        place, one_kept, one_sent, z_first, [b for b in left if b != 2], piece, {len(z_first) - 2: (two_sent[-1],)}
    )
    first_wgrad, group_wgrad = last_of(place, normalizer, *one, *two, channels, TAPS * gw)
    return (input_grad.reshape(outer_grad.shape), third_wgrad, group_wgrad, first_wgrad)


def solution(mesh):
    tiles = P(("parts", "space"), None, None, None)
    rows = P(("parts", "space"), None)
    return jax.shard_map(
        per_device,
        mesh=mesh,
        in_specs=(tiles, tiles, tiles, tiles, P(), P(), P()),
        out_specs=(tiles, rows, rows, rows),
        check_vma=False,
    )
```
